256 devices in a mesh: head: 16 (over y_lo, x, core), seq: 16 (over z, y_hi).
Axes of the slice: x: 4, y: 4 (y_hi: 2, y_lo: 2; y = y_hi * 2 + y_lo), z: 8, core: 2. Of those that a mesh axis runs over, the one named last changes fastest.
Arguments:
- layer_input: bfloat16 [8192, 2048], P('seq'), may hold values from -6 to 6
- qkv_weight: bfloat16 [3, 2048, 2048], P(None, None, 'head'), may hold values from -0.1875 to 0.1875
- queries: bfloat16 [8192, 2048], P('seq', 'head'), may hold values from -6 to 6
- key_states: bfloat16 [8192, 2048], P('seq', 'head'), may hold values from -6 to 6
- value_states: bfloat16 [8192, 2048], P('seq', 'head'), may hold values from -6 to 6
- attn_out: bfloat16 [8192, 2048], P('seq', 'head'), may hold values from -4 to 4
- grad_out: bfloat16 [8192, 2048], P('seq', 'head'), may hold values from -24 to 24
- log_sum_exp: float32 [8192, 32], P('seq', 'head'), as said below
- frames: int32 [128], replicated, may hold values from 0 to 31, as said below
Outputs:
- input_grad: bfloat16 [8192, 2048], P('seq', 'head')
- weight_grad: float32 [3, 2048, 2048], P(None, 'seq', 'head')
The draws below stay inside these ranges and needn't reach their ends.
Inputs may be any that keep to these rules, and one draw needn't show every extreme that they name: frames[0] is 0 and each next block has the same frame or the next one; there are exactly 32 frames of varying lengths. `log_sum_exp`: each entry lies within 0.75 of ln(n) + 0.5, where n is the number of keys visible to its token.
All inputs are finite; a program needn't handle non-finite values.
Results may differ from the reference program's by a relative error of at most 0.025.
Values may be sent and summed in bfloat16 or wider, within the bound.
A program may use at most 64 MiB of HBM per device.

```python
import jax
import jax.numpy as jnp
from jax import lax

D = 2048
HEADS = 32
HEAD_DIM = 64
BLOCK = 64
TOKENS = 8192
FRAMES = 32
N_HEAD = 16


def frame_ids(key):
    shared = jax.random.fold_in(key, 11)
    block_total = TOKENS // BLOCK
    order = jax.random.permutation(shared, block_total - 1) + 1
    cut_points = order[:FRAMES - 1]
    starts = jnp.zeros((block_total,), jnp.int32).at[cut_points].set(1)
    return jnp.cumsum(starts).astype(jnp.int32)


def draw_frames(key, part):
    block_ids = frame_ids(key)
    return block_ids


def draw_log_sum_exp(key, part):
    block_ids = frame_ids(key)
    key = jax.random.fold_in(key, 5)
    seen_blocks = jnp.sum((block_ids[None, :] <= block_ids[:, None]).astype(jnp.int32), axis=1)
    visible_keys = jnp.repeat(seen_blocks * BLOCK, BLOCK, total_repeat_length=TOKENS)
    center = jnp.log(visible_keys.astype(jnp.float32)) + 0.5
    offset = jax.random.uniform(key, (TOKENS, HEADS), jnp.float32, -0.75, 0.75)
    return center[:, None] + offset


def spiked(result, stream_key, source, target, shards_of, factor):
    owner, partner = [(jnp.arange(result.shape[axis_at]) // (result.shape[axis_at] // shards_of)).reshape([-1 if axis == axis_at else 1 for axis in range(result.ndim)]) for axis_at in (source, target)]
    chosen = jax.random.permutation(stream_key, shards_of)[partner]
    strong = (owner == chosen) | (owner == (partner + shards_of // 2) % shards_of)
    return jnp.where(strong, factor * result, result)


def block_scale(own_key, dims, cuts, smallest, top_value):
    def one(axis_at, shards_of):
        steps = jax.random.uniform(jax.random.fold_in(jax.random.fold_in(own_key, 6), axis_at), (shards_of,), jnp.float32, smallest / len(cuts), top_value / len(cuts))
        return jnp.repeat(jnp.exp(steps), dims[axis_at] // shards_of).reshape((-1,) + (1,) * (len(dims) - axis_at - 1))

    level = one(*cuts[0])
    for cut in cuts[1:]:
        level = level * one(*cut)
    return level


def noise(stream_key, extent, width, reach, pieces=(), held_as=jnp.bfloat16):
    values = width * jax.random.normal(stream_key, extent, jnp.float32)
    if pieces:
        values = values * block_scale(stream_key, extent, pieces, -0.22, 0.18)
    return jnp.clip(values, -reach, reach).astype(held_as)


def bell_draw_with(stream_key, extent, scale, bound, pieces, heavy, held_as=jnp.bfloat16):
    values = scale * jax.random.normal(stream_key, extent, jnp.float32)
    if pieces:
        values = values * block_scale(stream_key, extent, pieces, -0.22, 0.18)
    return jnp.clip(spiked(values, jax.random.fold_in(stream_key, 3), *heavy), -bound, bound).astype(held_as)


def setup_inputs(seed: int = 0) -> dict:
    key_list = jax.random.split(jax.random.key(seed), 10)
    layer_input = noise(key_list[0], (TOKENS, D), 1.0, 6.0, ((0, 16),))
    qkv_weight = bell_draw_with(key_list[1], (3, D, D), D ** -0.5, 0.1875, ((2, 16),), (2, 1, 16, 2.0))
    queries = noise(key_list[2], (TOKENS, D), 1.0, 6.0, ((0, 16), (1, 16)))
    key_states = noise(key_list[3], (TOKENS, D), 1.0, 6.0, ((0, 16), (1, 16)))
    value_states = noise(key_list[4], (TOKENS, D), 1.0, 6.0, ((0, 16), (1, 16)))
    attn_out = noise(key_list[5], (TOKENS, D), 0.5, 4.0, ((0, 16), (1, 16)))
    grad_out = noise(key_list[6], (TOKENS, D), 4.0, 24.0, ((0, 16), (1, 16)))
    log_sum_exp = draw_log_sum_exp(jax.random.fold_in(key_list[9], 71), 0)
    frames = draw_frames(jax.random.fold_in(key_list[9], 71), 0)
    return dict(layer_input=layer_input, qkv_weight=qkv_weight, queries=queries, key_states=key_states, value_states=value_states, attn_out=attn_out, grad_out=grad_out, log_sum_exp=log_sum_exp, frames=frames)


def product(left, right):
    return jnp.dot(left, right, preferred_element_type=jnp.float32, precision=lax.Precision.HIGHEST)


def rounded_low(value):
    return lax.optimization_barrier(value.astype(jnp.bfloat16)).astype(jnp.float32)


def reference(layer_input, qkv_weight, queries, key_states, value_states, attn_out, grad_out, log_sum_exp, frames):
    total_rows = queries.shape[0]
    score_scale = HEAD_DIM ** -0.5
    token_frames = jnp.repeat(frames, BLOCK, total_repeat_length=total_rows)
    row_delta = jnp.sum((grad_out.astype(jnp.float32) * attn_out.astype(jnp.float32)).reshape(total_rows, HEADS, HEAD_DIM), axis=2)

    def by_head(array):
        return array.reshape(total_rows, HEADS, HEAD_DIM).transpose(1, 0, 2).astype(jnp.float32)

    block_rows = min(1024, total_rows)

    def one_head(operands):
        query_head, key_head, value_head, grad_head, stat_head, delta_head = operands

        def query_step(running, block_index):
            row_start = block_index * block_rows
            query_part = lax.dynamic_slice_in_dim(query_head, row_start, block_rows, 0)
            grad_part = lax.dynamic_slice_in_dim(grad_head, row_start, block_rows, 0)
            stat_part = lax.dynamic_slice_in_dim(stat_head, row_start, block_rows, 0)
            delta_part = lax.dynamic_slice_in_dim(delta_head, row_start, block_rows, 0)
            query_frames = lax.dynamic_slice_in_dim(token_frames, row_start, block_rows, 0)
            visible = token_frames[None, :] <= query_frames[:, None]
            scores = product(query_part, key_head.T)
            probs = jnp.where(visible, jnp.exp(scores * score_scale - stat_part[:, None]), 0.0)
            value_grad = running[1] + product(rounded_low(probs).T, grad_part)
            prob_grad = product(grad_part, value_head.T)
            score_grad = rounded_low(probs * (prob_grad - delta_part[:, None]))
            query_grad = product(score_grad, key_head) * score_scale
            key_grad = running[0] + product(score_grad.T, query_part) * score_scale
            return (key_grad, value_grad), query_grad

        empty = jnp.zeros((total_rows, HEAD_DIM), jnp.float32)
        (key_grad, value_grad), query_grad = lax.scan(query_step, (empty, empty), jnp.arange(total_rows // block_rows, dtype=jnp.int32))
        return query_grad.reshape(total_rows, HEAD_DIM), key_grad, value_grad

    per_head = lax.map(one_head, (by_head(queries), by_head(key_states), by_head(value_states), by_head(grad_out), log_sum_exp.T, row_delta.T))

    def merged(array):
        return array.transpose(1, 0, 2).reshape(total_rows, HEADS * HEAD_DIM).astype(jnp.bfloat16)

    grads = jnp.stack([merged(member) for member in per_head])
    wide_input = layer_input.astype(jnp.float32)
    weight_grad = jnp.stack([product(wide_input.T, grads[member].astype(jnp.float32)) for member in range(3)])
    group_width = D // N_HEAD

    def group_step(running, group_index):
        group_grads = lax.dynamic_slice_in_dim(grads, group_index * group_width, group_width, 2).astype(jnp.float32)
        group_weights = lax.dynamic_slice_in_dim(qkv_weight, group_index * group_width, group_width, 2).astype(jnp.float32)
        partial_value = jnp.einsum("mtc,mdc->td", group_grads, group_weights, precision=lax.Precision.HIGHEST)
        return running + rounded_low(partial_value), None

    input_total, unused = lax.scan(group_step, jnp.zeros((total_rows, D), jnp.float32), jnp.arange(N_HEAD, dtype=jnp.int32))
    return input_total.astype(jnp.bfloat16), weight_grad
```

```python
import functools

import jax
import jax.numpy as jnp
from jax import lax
from jax.experimental import pallas as pl
from jax.experimental.pallas import tpu as pltpu
from jax.sharding import PartitionSpec as P

BLOCK = 64
HEAD_SIZE = 64
COLS = 2 * HEAD_SIZE
FRAMES = 32
CHUNK = 256
HIDDEN = -16384.0
LOG2E = 1.4426950408889634
MESH = pl.DeviceIdType.MESH
BF16 = jnp.bfloat16
F32 = jnp.float32


def dot(left, right):
    return jnp.dot(left, right, preferred_element_type=F32)


def dot_nt(left, right):
    return lax.dot_general(left, right, (((1,), (1,)), ((), ())), preferred_element_type=F32)


def greet(peers):
    barrier = pltpu.get_barrier_semaphore()
    for peer in peers:
        pl.semaphore_signal(barrier, inc=1, device_id=peer, device_id_type=MESH)
    pl.semaphore_wait(barrier, len(peers))


def remote(source, target, send_sem, recv_sem, peer):
    return pltpu.make_async_remote_copy(
        src_ref=source,
        dst_ref=target,
        send_sem=send_sem,
        recv_sem=recv_sem,
        device_id=peer,
        device_id_type=MESH,
    )


def attention_kernel(
    nz,
    frames_ref,
    stat_ref,
    query_ref,
    key_ref,
    value_ref,
    out_ref,
    grad_ref,
    grads_ref,
    flipped_ref,
    key_other,
    value_other,
    slots,
    trail_send,
    trail_recv,
    key_wide,
    value_wide,
    key_flip,
    fixed,
    paired,
    score_low,
    key_sum,
    value_sum,
    own_query,
    part_send,
    part_recv,
    slot_sems,
    trail_sems,
    pair_sems,
):
    rows = query_ref.shape[0]
    half = rows // 2
    blocks = rows // BLOCK
    seq = lax.axis_index("seq")
    count = 2 * nz
    side = lax.rem(seq, 2)
    partner = seq + 1 - 2 * side
    up = lax.rem(seq + 2, count)
    down = lax.rem(seq + count - 2, count)
    ahead = ({"seq": up}, {"seq": down})
    greet(({"seq": partner}, {"seq": up}, {"seq": down}))

    pair_copies = [
        remote(key_ref, key_other, pair_sems.at[0, 0], pair_sems.at[1, 0], {"seq": partner}),
        remote(value_ref, value_other, pair_sems.at[0, 1], pair_sems.at[1, 1], {"seq": partner}),
    ]
    for copy in pair_copies:
        copy.start()

    def slot_copy(r, t):
        return remote(
            slots.at[r, t],
            slots.at[r, t + 1],
            slot_sems.at[0, r, t],
            slot_sems.at[1, r, t + 1],
            ahead[r],
        )

    def trail_copy(r, t):
        return remote(
            trail_send.at[r, t],
            trail_recv.at[r, t + 1],
            trail_sems.at[0, r, t],
            trail_sems.at[1, r, t + 1],
            ahead[r],
        )

    grad_wide = grad_ref[...].astype(F32)
    query_flip = jnp.transpose(query_ref[...].astype(F32) * (HEAD_SIZE**-0.5))
    grad_flip = jnp.transpose(grad_wide)
    delta_flip = jnp.transpose(grad_wide * out_ref[...].astype(F32))
    aux_row = lax.broadcasted_iota(jnp.int32, (16, rows), 0)
    aux = jnp.zeros((16, rows), F32)
    for h in range(2):
        delta = jnp.sum(
            delta_flip[h * HEAD_SIZE : (h + 1) * HEAD_SIZE, :], axis=0, keepdims=True
        )
        for first, value in ((3 * h, stat_ref[h : h + 1, :]), (6 + 3 * h, delta)):
            rest = value
            for place in range(3):
                piece = rest.astype(BF16).astype(F32)
                aux = jnp.where(aux_row == first + place, piece, aux)
                rest = rest - piece
    for r in range(2):
        lanes = slice(r * half, (r + 1) * half)
        slots[r, 0, 0:COLS, :] = query_flip[:, lanes].astype(BF16)
        slots[r, 0, COLS : 2 * COLS, :] = grad_flip[:, lanes].astype(BF16)
        slots[r, 0, 2 * COLS : 2 * COLS + 16, :] = aux[:, lanes].astype(BF16)
        slot_copy(r, 0).start()

    lane = lax.broadcasted_iota(jnp.int32, (BLOCK, COLS), 1)
    inner = lax.rem(lane, HEAD_SIZE)

    def build_keys(keys_from, values_from, base, owner):
        for b in range(blocks):
            here = slice(b * BLOCK, (b + 1) * BLOCK)
            there = slice(base + b * BLOCK, base + (b + 1) * BLOCK)
            frame = frames_ref[owner * blocks + b]
            keys = keys_from[here, :].astype(F32)
            values = values_from[here, :].astype(F32)
            for h in range(2):
                mine = (lane >= h * HEAD_SIZE) & (lane < (h + 1) * HEAD_SIZE)
                stat_at = (inner >= FRAMES + 3 * h) & (inner < FRAMES + 3 * h + 3)
                delta_at = (inner >= FRAMES + 6 + 3 * h) & (inner < FRAMES + 9 + 3 * h)
                key_more = jnp.where(inner == frame, 1.0, jnp.where(stat_at, -1.0, 0.0))
                value_more = jnp.where(delta_at, -1.0, 0.0)
                key_wide[h, there, :] = jnp.where(mine, keys, key_more).astype(BF16)
                value_wide[h, there, :] = jnp.where(mine, values, value_more).astype(BF16)
        key_flip[:, base : base + rows] = jnp.transpose(
            keys_from[...].astype(F32) * (HEAD_SIZE**-0.5)
        ).astype(BF16)

    frame_row = lax.broadcasted_iota(jnp.int32, (FRAMES, half), 0)
    frame_lane = lax.broadcasted_iota(jnp.int32, (FRAMES, half), 1)

    def prepare(r, t, owner):
        first = owner * blocks + r * (blocks // 2)
        seen = jnp.full((FRAMES, half), frames_ref[first + blocks // 2 - 1], jnp.int32)
        for i in range(blocks // 2 - 2, -1, -1):
            seen = jnp.where(frame_lane < (i + 1) * BLOCK, frames_ref[first + i], seen)
        hidden = jnp.where(frame_row > seen, HIDDEN, 0.0).astype(BF16)
        extra = jnp.concatenate(
            [hidden, slots[r, t, 2 * COLS : 2 * COLS + 16, :], jnp.zeros((16, half), BF16)], axis=0
        )
        zero = jnp.zeros((HEAD_SIZE, half), BF16)
        for which in range(2):
            low = slots[r, t, which * COLS : which * COLS + HEAD_SIZE, :]
            high = slots[r, t, which * COLS + HEAD_SIZE : (which + 1) * COLS, :]
            fixed[r, 2 * which, :, :] = jnp.concatenate([low, extra], axis=0)
            fixed[r, 2 * which + 1, :, :] = jnp.concatenate([extra, high], axis=0)
            paired[r, which, :, :] = jnp.concatenate(
                [jnp.concatenate([low, zero], axis=1), jnp.concatenate([zero, high], axis=1)], axis=0
            )

    def tile(r, start):
        here = pl.ds(start, CHUNK)
        probs, scores = [], []
        for h in range(2):
            score = dot(key_wide[h, here, :], fixed[r, h, :, :])
            prob = jnp.exp2(score * LOG2E)
            prob_grad = dot(value_wide[h, here, :], fixed[r, 2 + h, :, :])
            score_grad = (prob * prob_grad).astype(BF16)
            score_low[r, h, here, :] = score_grad
            probs.append(prob.astype(BF16))
            scores.append(score_grad)
        value_sum[here, :] += dot_nt(jnp.concatenate(probs, axis=1), paired[r, 1, :, :])
        key_sum[here, :] += dot_nt(jnp.concatenate(scores, axis=1), paired[r, 0, :, :])

    def tiles(first):
        for c in range(rows // CHUNK):
            for r in range(2):
                tile(r, pl.multiple_of(first + c * CHUNK, CHUNK))

    def query_part(r):
        return jnp.concatenate(
            [
                dot(key_flip[h * HEAD_SIZE : (h + 1) * HEAD_SIZE, :], score_low[r, h, :, :])
                for h in range(2)
            ],
            axis=0,
        )

    key_sum[...] = jnp.zeros_like(key_sum)
    value_sum[...] = jnp.zeros_like(value_sum)
    for r in range(2):
        trail_recv[r, 1, :, :] = jnp.zeros((COLS, half), BF16)
        prepare(r, 0, seq)
    build_keys(key_ref, value_ref, 0, seq)
    tiles(0)
    for copy in pair_copies:
        copy.wait()
    build_keys(key_other, value_other, rows, partner)
    tiles(rows)
    for r in range(2):
        own_query[:, r * half : (r + 1) * half] = query_part(r)

    def step(t, carry):
        for r in range(2):
            slot_copy(r, t - 1).wait_recv()

        @pl.when(t < nz - 1)
        def _():
            for r in range(2):
                slot_copy(r, t).start()

        prepare(0, t, lax.rem(seq + 2 * (nz - t), count))
        prepare(1, t, lax.rem(seq + 2 * t, count))

        def part(i, inner_carry):
            tiles(i * rows)
            return inner_carry

        lax.fori_loop(0, 2, part, 0)

        @pl.when(t > 1)
        def _():
            for r in range(2):
                trail_copy(r, t - 1).wait_recv()

        for r in range(2):
            total = query_part(r) + trail_recv[r, t, :, :].astype(F32)
            trail_send[r, t, :, :] = total.astype(BF16)
            trail_copy(r, t).start()
        return carry

    lax.fori_loop(1, nz, step, 0)

    part_send[0, :, :] = key_sum[rows:, :].astype(BF16)
    part_send[1, :, :] = value_sum[rows:, :].astype(BF16)
    part_copy = remote(part_send, part_recv, pair_sems.at[0, 2], pair_sems.at[1, 2], {"seq": partner})
    part_copy.start()

    for r in range(2):
        trail_copy(r, nz - 1).wait_recv()
        lanes = slice(r * half, (r + 1) * half)
        own_query[:, lanes] += trail_recv[r, nz, :, :].astype(F32)
    query_low = own_query[...].astype(BF16)
    flipped_ref[0:COLS, :] = query_low
    grads_ref[:, 0:COLS] = jnp.transpose(query_low.astype(F32)).astype(BF16)
    part_copy.wait_recv()
    for m, total in ((1, key_sum), (2, value_sum)):
        low = (total[0:rows, :] + part_recv[m - 1, :, :].astype(F32)).astype(BF16)
        grads_ref[:, m * COLS : (m + 1) * COLS] = low
        flipped_ref[m * COLS : (m + 1) * COLS, :] = jnp.transpose(low.astype(F32)).astype(BF16)

    part_copy.wait_send()
    for r in range(2):

        def drain(t, carry, r=r):
            slot_copy(r, t).wait_send()
            trail_copy(r, t + 1).wait_send()
            return carry

        lax.fori_loop(0, nz - 1, drain, 0)


def projection_kernel(
    nz,
    nx,
    input_ref,
    weight_ref,
    grads_ref,
    flipped_ref,
    input_out,
    weight_out,
    core_send,
    core_recv,
    x_send,
    x_recv,
    y_send,
    y_recv,
    z_send,
    z_recv,
    yh_send,
    yh_recv,
    core_sems,
    x_sems,
    y_sems,
    z_sems,
    yh_sems,
):
    seq = lax.axis_index("seq")
    head = lax.axis_index("head")
    count = 2 * nz
    side = lax.rem(seq, 2)
    z = seq // 2
    partner = {"seq": seq + 1 - 2 * side}
    z_ahead = ({"seq": lax.rem(seq + 2, count)}, {"seq": lax.rem(seq + count - 2, count)})
    core = lax.rem(head, 2)
    x = lax.rem(head // 2, nx)
    low_side = head // (2 * nx)
    twin = {"head": head + 1 - 2 * core}
    plane = low_side * 2 * nx + core
    x_ahead = (
        {"head": plane + 2 * lax.rem(x + 1, nx)},
        {"head": plane + 2 * lax.rem(x + nx - 1, nx)},
    )
    neighbour = {"head": (1 - low_side) * 2 * nx + 2 * x + core}
    greet((partner, *z_ahead, twin, *x_ahead, neighbour))

    def input_term(x_at, y_at, core_at):
        first = pl.multiple_of(((y_at * nx + x_at) * 2 + core_at) * COLS, COLS)
        weights = jnp.concatenate(
            [weight_ref[m, pl.ds(first, COLS), :] for m in range(3)], axis=1
        )
        return dot_nt(grads_ref[...], weights)

    def weight_term(z_at, side_at):
        first = pl.multiple_of((z_at * 2 + side_at) * COLS, COLS)
        return dot(flipped_ref[...], input_ref[:, pl.ds(first, COLS)])

    def reach(length, i):
        return (length - i) // 2

    def at(r, distance, position, length):
        return lax.rem(position + distance if r == 0 else position + length - distance, length)

    def half_of(r, i):
        return (i + r) % 2

    core_order = [(r, i) for i in range(nx - 1) for r in range(2)] + [(0, nx - 1), (0, nx)]
    core_copies = {}
    for place, (r, i) in enumerate(core_order):
        x_at = at(r, reach(nx, i), x, nx)
        y_at = half_of(r, i)
        core_send[place, :, :] = input_term(x_at, y_at, 1 - core).astype(BF16)
        copy = remote(
            core_send.at[place],
            core_recv.at[place],
            core_sems.at[0, place],
            core_sems.at[1, place],
            twin,
        )
        copy.start()
        core_copies[r, i] = (place, copy)

    started = [copy for _, copy in core_copies.values()]

    z_copies = {}

    def z_message(i):
        for r in range(2):
            total = weight_term(at(r, reach(nz, i), z, nz), half_of(r, i))
            if i >= 2:
                z_copies[r, i - 2].wait_recv()
                total = total + z_recv[r, i - 2, :, :].astype(F32)
            z_send[r, i, :, :] = total.astype(BF16)
            copy = remote(
                z_send.at[r, i], z_recv.at[r, i], z_sems.at[0, r, i], z_sems.at[1, r, i], z_ahead[r]
            )
            copy.start()
            z_copies[r, i] = copy
            started.append(copy)

    x_copies = {}

    def input_pair(r, i):
        place, copy = core_copies[r, i]
        total = input_term(at(r, reach(nx, i), x, nx), half_of(r, i), core)
        copy.wait_recv()
        return total + core_recv[place, :, :].astype(F32)

    def x_message(i):
        for r in range(2):
            total = input_pair(r, i)
            if i >= 2:
                x_copies[r, i - 2].wait_recv()
                total = total + x_recv[r, i - 2, :, :].astype(F32)
            x_send[r, i, :, :] = total.astype(BF16)
            copy = remote(
                x_send.at[r, i], x_recv.at[r, i], x_sems.at[0, r, i], x_sems.at[1, r, i], x_ahead[r]
            )
            copy.start()
            x_copies[r, i] = copy
            started.append(copy)

    def x_final(place):
        total = input_pair(0, nx - 1 + place)
        y_at = half_of(0, nx - 1 + place)
        for r in range(2):
            i = nx - 2 if half_of(r, nx - 2) == y_at else nx - 3
            x_copies[r, i].wait_recv()
            total = total + x_recv[r, i, :, :].astype(F32)
        return y_at, total

    def z_final(side_at):
        total = weight_term(z, side_at)
        for r in range(2):
            i = nz - 2 if half_of(r, nz - 2) == side_at else nz - 3
            z_copies[r, i].wait_recv()
            total = total + z_recv[r, i, :, :].astype(F32)
        return total

    z_message(0)
    z_message(1)
    x_message(0)
    x_message(1)
    z_message(2)
    x_message(2)
    z_message(3)
    finals = dict(x_final(place) for place in range(2))
    mine = jnp.where(low_side == 0, finals[0], finals[1])
    y_send[...] = jnp.where(low_side == 0, finals[1], finals[0]).astype(BF16)
    y_copy = remote(y_send, y_recv, y_sems.at[0], y_sems.at[1], neighbour)
    y_copy.start()
    for i in range(4, nz - 1):
        z_message(i)
    y_copy.wait_recv()
    input_out[...] = (mine + y_recv[...].astype(F32)).astype(BF16)
    sides = [z_final(side_at) for side_at in range(2)]
    kept = jnp.where(side == 0, sides[0], sides[1])
    yh_send[...] = jnp.where(side == 0, sides[1], sides[0]).astype(BF16)
    yh_copy = remote(yh_send, yh_recv, yh_sems.at[0], yh_sems.at[1], partner)
    yh_copy.start()
    yh_copy.wait_recv()
    total = kept + yh_recv[...].astype(F32)
    for m in range(3):
        weight_out[m, :, :] = jnp.transpose(total[m * COLS : (m + 1) * COLS, :])
    y_copy.wait_send()
    yh_copy.wait_send()
    for copy in started:
        copy.wait_send()


def local(
    nz,
    nx,
    layer_input,
    qkv_weight,
    queries,
    key_states,
    value_states,
    attn_out,
    grad_out,
    log_sum_exp,
    frames,
):
    rows = queries.shape[0]
    half = rows // 2
    vmem = pl.BlockSpec(memory_space=pltpu.VMEM)
    smem = pl.BlockSpec(memory_space=pltpu.SMEM)
    dma = pltpu.SemaphoreType.DMA
    grads, flipped = pl.pallas_call(
        functools.partial(attention_kernel, nz),
        out_shape=(
            jax.ShapeDtypeStruct((rows, 3 * COLS), BF16),
            jax.ShapeDtypeStruct((3 * COLS, rows), BF16),
        ),
        in_specs=[smem] + [vmem] * 6,
        out_specs=(vmem, vmem),
        scratch_shapes=[
            pltpu.VMEM((rows, COLS), BF16),
            pltpu.VMEM((rows, COLS), BF16),
            pltpu.VMEM((2, nz, 2 * COLS + 16, half), BF16),
            pltpu.VMEM((2, nz, COLS, half), BF16),
            pltpu.VMEM((2, nz + 1, COLS, half), BF16),
            pltpu.VMEM((2, 2 * rows, COLS), BF16),
            pltpu.VMEM((2, 2 * rows, COLS), BF16),
            pltpu.VMEM((COLS, 2 * rows), BF16),
            pltpu.VMEM((2, 4, COLS, half), BF16),
            pltpu.VMEM((2, 2, COLS, 2 * half), BF16),
            pltpu.VMEM((2, 2, 2 * rows, half), BF16),
            pltpu.VMEM((2 * rows, COLS), F32),
            pltpu.VMEM((2 * rows, COLS), F32),
            pltpu.VMEM((COLS, rows), F32),
            pltpu.VMEM((2, rows, COLS), BF16),
            pltpu.VMEM((2, rows, COLS), BF16),
            dma((2, 2, nz)),
            dma((2, 2, nz + 1)),
            dma((2, 3)),
        ],
        compiler_params=pltpu.CompilerParams(
            collective_id=0, has_side_effects=True, vmem_limit_bytes=48 * 2**20
        ),
        name="attention_ring",
    )(frames, log_sum_exp.T, queries, key_states, value_states, attn_out, grad_out)
    wide = 3 * COLS
    input_grad, weight_grad = pl.pallas_call(
        functools.partial(projection_kernel, nz, nx),
        out_shape=(
            jax.ShapeDtypeStruct((rows, COLS), BF16),
            jax.ShapeDtypeStruct((3, COLS, COLS), F32),
        ),
        in_specs=[vmem] * 4,
        out_specs=(vmem, vmem),
        scratch_shapes=[
            pltpu.VMEM((2 * nx, rows, COLS), BF16),
            pltpu.VMEM((2 * nx, rows, COLS), BF16),
            pltpu.VMEM((2, nx - 1, rows, COLS), BF16),
            pltpu.VMEM((2, nx - 1, rows, COLS), BF16),
            pltpu.VMEM((rows, COLS), BF16),
            pltpu.VMEM((rows, COLS), BF16),
            pltpu.VMEM((2, nz - 1, wide, COLS), BF16),
            pltpu.VMEM((2, nz - 1, wide, COLS), BF16),
            pltpu.VMEM((wide, COLS), BF16),
            pltpu.VMEM((wide, COLS), BF16),
            dma((2, 2 * nx)),
            dma((2, 2, nx - 1)),
            dma((2,)),
            dma((2, 2, nz - 1)),
            dma((2,)),
        ],
        compiler_params=pltpu.CompilerParams(
            collective_id=1, has_side_effects=True, vmem_limit_bytes=48 * 2**20
        ),
        name="projection_sums",
    )(layer_input, qkv_weight, grads, flipped)
    return input_grad, weight_grad


def solution(mesh):
    nz = mesh.shape["seq"] // 2
    nx = mesh.shape["head"] // 4
    placed = (
        P("seq", None),
        P(None, None, "head"),
        P("seq", "head"),
        P("seq", "head"),
        P("seq", "head"),
        P("seq", "head"),
        P("seq", "head"),
        P("seq", "head"),
        P(),
    )
    return jax.shard_map(
        functools.partial(local, nz, nx),
        mesh=mesh,
        in_specs=placed,
        out_specs=(P("seq", "head"), P(None, "seq", "head")),
        check_vma=False,
    )
```

```python
import functools

import jax
import jax.numpy as jnp
from jax import lax
from jax.experimental import pallas as pl
from jax.experimental.pallas import tpu as pltpu
from jax.sharding import PartitionSpec as P

BLOCK = 64
HEAD_SIZE = 64
COLS = 2 * HEAD_SIZE
FRAMES = 32
CHUNK = 256
HIDDEN = -16384.0
LOG2E = 1.4426950408889634
MESH = pl.DeviceIdType.MESH
BF16 = jnp.bfloat16
F32 = jnp.float32


def dot(left, right):
    return jnp.dot(left, right, preferred_element_type=F32)


def dot_nt(left, right):
    return lax.dot_general(left, right, (((1,), (1,)), ((), ())), preferred_element_type=F32)


def greet(peers):
    barrier = pltpu.get_barrier_semaphore()
    for peer in peers:
        pl.semaphore_signal(barrier, inc=1, device_id=peer, device_id_type=MESH)
    pl.semaphore_wait(barrier, len(peers))


def remote(source, target, send_sem, recv_sem, peer):
    return pltpu.make_async_remote_copy(
        src_ref=source,
        dst_ref=target,
        send_sem=send_sem,
        recv_sem=recv_sem,
        device_id=peer,
        device_id_type=MESH,
    )


def backward_kernel(
    nz,
    nx,
    frames_hbm,
    stat_hbm,
    query_hbm,
    key_hbm,
    value_hbm,
    out_hbm,
    grad_hbm,
    input_hbm,
    weight_hbm,
    input_out,
    weight_out,
    frames_ref,
    stat_ref,
    query_ref,
    key_ref,
    value_ref,
    out_ref,
    grad_ref,
    input_ref,
    weight_ref,
    key_other,
    value_other,
    slots,
    trail_send,
    trail_recv,
    key_wide,
    value_wide,
    key_flip,
    fixed,
    paired,
    score_low,
    key_sum,
    value_sum,
    early_query,
    part_send,
    part_recv,
    grads_ref,
    flipped_ref,
    core_send,
    core_recv,
    x_send,
    x_recv,
    y_send,
    y_recv,
    zq_send,
    zq_recv,
    zk_send,
    zk_recv,
    yh_send,
    yh_recv,
    load_sems,
    slot_sems,
    trail_sems,
    pair_sems,
    part_sems,
    core_sems,
    x_sems,
    y_sems,
    z_sems,
    yh_sems,
):
    loads = [
        pltpu.make_async_copy(source, target, load_sems.at[i])
        for i, (source, target) in enumerate(
            (
                (grad_hbm, grad_ref),
                (query_hbm, query_ref),
                (out_hbm, out_ref),
                (stat_hbm, stat_ref),
                (key_hbm, key_ref),
                (value_hbm, value_ref),
                (frames_hbm, frames_ref),
                (input_hbm, input_ref),
                (weight_hbm, weight_ref),
            )
        )
    ]
    for load in loads:
        load.start()

    rows = query_ref.shape[0]
    half = rows // 2
    blocks = rows // BLOCK
    count = 2 * nz
    seq = lax.axis_index("seq")
    head = lax.axis_index("head")
    side = lax.rem(seq, 2)
    z = seq // 2
    partner_seq = seq + 1 - 2 * side
    partner = {"seq": partner_seq}
    z_ahead = ({"seq": lax.rem(seq + 2, count)}, {"seq": lax.rem(seq + count - 2, count)})
    core = lax.rem(head, 2)
    x = lax.rem(head // 2, nx)
    low_side = head // (2 * nx)
    twin = {"head": head + 1 - 2 * core}
    plane = low_side * 2 * nx + core
    x_ahead = (
        {"head": plane + 2 * lax.rem(x + 1, nx)},
        {"head": plane + 2 * lax.rem(x + nx - 1, nx)},
    )
    low_head = (1 - low_side) * 2 * nx + 2 * x + core
    neighbour = {"head": low_head}
    y_ahead = (
        {"seq": seq + low_side * (partner_seq - seq), "head": low_head},
        {"seq": partner_seq + low_side * (seq - partner_seq), "head": low_head},
    )
    greet((partner, *z_ahead, twin, *x_ahead, *y_ahead))

    pair_copies = [
        remote(key_hbm, key_other, pair_sems.at[0, 0], pair_sems.at[1, 0], partner),
        remote(value_hbm, value_other, pair_sems.at[0, 1], pair_sems.at[1, 1], partner),
    ]
    for copy in pair_copies:
        copy.start()

    def slot_copy(r, t, part):
        here = pl.ds(0, COLS) if part == 0 else pl.ds(COLS, COLS + 16)
        return remote(
            slots.at[r, t, here],
            slots.at[r, t + 1, here],
            slot_sems.at[0, part, r, t],
            slot_sems.at[1, part, r, t + 1],
            z_ahead[r],
        )

    def trail_copy(r, t):
        return remote(
            trail_send.at[r, t],
            trail_recv.at[r, t + 1],
            trail_sems.at[0, r, t],
            trail_sems.at[1, r, t + 1],
            z_ahead[r],
        )

    for load in loads[:4]:
        load.wait()
    grad_wide = grad_ref[...].astype(F32)
    query_flip = jnp.transpose(query_ref[...].astype(F32) * (HEAD_SIZE**-0.5))
    grad_flip = jnp.transpose(grad_wide)
    delta_flip = jnp.transpose(grad_wide * out_ref[...].astype(F32))
    aux_row = lax.broadcasted_iota(jnp.int32, (16, rows), 0)
    aux = jnp.zeros((16, rows), F32)
    for h in range(2):
        delta = jnp.sum(
            delta_flip[h * HEAD_SIZE : (h + 1) * HEAD_SIZE, :], axis=0, keepdims=True
        )
        for first, value in ((3 * h, stat_ref[h : h + 1, :]), (6 + 3 * h, delta)):
            rest = value
            for place in range(3):
                piece = rest.astype(BF16).astype(F32)
                aux = jnp.where(aux_row == first + place, piece, aux)
                rest = rest - piece
    for r in range(2):
        lanes = slice(r * half, (r + 1) * half)
        slots[r, 0, 0:COLS, :] = query_flip[:, lanes].astype(BF16)
        slots[r, 0, COLS : 2 * COLS, :] = grad_flip[:, lanes].astype(BF16)
        slots[r, 0, 2 * COLS : 2 * COLS + 16, :] = aux[:, lanes].astype(BF16)

    lane = lax.broadcasted_iota(jnp.int32, (BLOCK, COLS), 1)
    inner = lax.rem(lane, HEAD_SIZE)

    def build_keys(keys_from, values_from, base, owner):
        for b in range(blocks):
            here = slice(b * BLOCK, (b + 1) * BLOCK)
            there = slice(base + b * BLOCK, base + (b + 1) * BLOCK)
            frame = frames_ref[owner * blocks + b]
            keys = keys_from[here, :].astype(F32)
            values = values_from[here, :].astype(F32)
            for h in range(2):
                mine = (lane >= h * HEAD_SIZE) & (lane < (h + 1) * HEAD_SIZE)
                stat_at = (inner >= FRAMES + 3 * h) & (inner < FRAMES + 3 * h + 3)
                delta_at = (inner >= FRAMES + 6 + 3 * h) & (inner < FRAMES + 9 + 3 * h)
                key_more = jnp.where(inner == frame, 1.0, jnp.where(stat_at, -1.0, 0.0))
                value_more = jnp.where(delta_at, -1.0, 0.0)
                key_wide[h, there, :] = jnp.where(mine, keys, key_more).astype(BF16)
                value_wide[h, there, :] = jnp.where(mine, values, value_more).astype(BF16)
        key_flip[:, base : base + rows] = jnp.transpose(
            keys_from[...].astype(F32) * (HEAD_SIZE**-0.5)
        ).astype(BF16)

    frame_row = lax.broadcasted_iota(jnp.int32, (FRAMES, half), 0)
    frame_lane = lax.broadcasted_iota(jnp.int32, (FRAMES, half), 1)

    def prepare(t):
        for r, owner in enumerate((lax.rem(seq + 2 * (nz - t), count), lax.rem(seq + 2 * t, count))):
            first = owner * blocks + r * (blocks // 2)
            seen = jnp.full((FRAMES, half), frames_ref[first + blocks // 2 - 1], jnp.int32)
            for i in range(blocks // 2 - 2, -1, -1):
                seen = jnp.where(frame_lane < (i + 1) * BLOCK, frames_ref[first + i], seen)
            hidden = jnp.where(frame_row > seen, HIDDEN, 0.0).astype(BF16)
            extra = jnp.concatenate(
                [hidden, slots[r, t, 2 * COLS : 2 * COLS + 16, :], jnp.zeros((16, half), BF16)],
                axis=0,
            )
            zero = jnp.zeros((HEAD_SIZE, half), BF16)
            for which in range(2):
                low = slots[r, t, which * COLS : which * COLS + HEAD_SIZE, :]
                high = slots[r, t, which * COLS + HEAD_SIZE : (which + 1) * COLS, :]
                fixed[r, 2 * which, :, :] = jnp.concatenate([low, extra], axis=0)
                fixed[r, 2 * which + 1, :, :] = jnp.concatenate([extra, high], axis=0)
                paired[r, which, :, :] = jnp.concatenate(
                    [
                        jnp.concatenate([low, zero], axis=1),
                        jnp.concatenate([zero, high], axis=1),
                    ],
                    axis=0,
                )

    def tile(r, start):
        here = pl.ds(start, CHUNK)
        probs, scores = [], []
        for h in range(2):
            score = dot(key_wide[h, here, :], fixed[r, h, :, :])
            prob = jnp.exp2(score * LOG2E)
            prob_grad = dot(value_wide[h, here, :], fixed[r, 2 + h, :, :])
            score_grad = (prob * prob_grad).astype(BF16)
            score_low[r, h, here, :] = score_grad
            probs.append(prob.astype(BF16))
            scores.append(score_grad)
        value_sum[here, :] += dot_nt(jnp.concatenate(probs, axis=1), paired[r, 1, :, :])
        key_sum[here, :] += dot_nt(jnp.concatenate(scores, axis=1), paired[r, 0, :, :])

    def tiles(first):
        for c in range(rows // CHUNK):
            for r in range(2):
                tile(r, first + c * CHUNK)

    def query_part(r, first, length):
        return jnp.concatenate(
            [
                dot(
                    key_flip[h * HEAD_SIZE : (h + 1) * HEAD_SIZE, first : first + length],
                    score_low[r, h, first : first + length, :],
                )
                for h in range(2)
            ],
            axis=0,
        )

    def receive(t, part):
        for r in range(2):
            slot_copy(r, t - 1, part).wait_recv()

    def forward(t, part):
        for r in range(2):
            slot_copy(r, t, part).start()

    def pass_on(t, part):
        receive(t, part)
        forward(t, part)

    def hand_on(t, totals):
        @pl.when(t > 1)
        def _():
            for r in range(2):
                trail_copy(r, t - 1).wait_recv()

        for r in range(2):
            total = totals[r] + trail_recv[r, t, :, :].astype(F32)
            trail_send[r, t, :, :] = total.astype(BF16)
            trail_copy(r, t).start()

    early = min(3, nz - 1)
    forward(0, 0)
    forward(0, 1)
    for load in loads[4:7]:
        load.wait()
    build_keys(key_ref, value_ref, 0, seq)
    key_sum[...] = jnp.zeros_like(key_sum)
    value_sum[...] = jnp.zeros_like(value_sum)
    for r in range(2):
        trail_recv[r, 1, :, :] = jnp.zeros((COLS, half), BF16)

    def own_step(t, carry):
        @pl.when(t > 0)
        def _():
            pass_on(t, 0)
            pass_on(t, 1)

        prepare(t)
        tiles(0)
        for r in range(2):
            early_query[r, t, :, :] = query_part(r, 0, rows)
        return carry

    lax.fori_loop(0, early, own_step, 0)
    for copy in pair_copies:
        copy.wait()
    build_keys(key_other, value_other, rows, partner_seq)

    def other_step(t, carry):
        prepare(t)
        tiles(rows)
        totals = [early_query[r, t, :, :] + query_part(r, rows, rows) for r in range(2)]

        @pl.when(t == 0)
        def _():
            for r in range(2):
                early_query[r, 0, :, :] = totals[r]

        @pl.when(t > 0)
        def _():
            hand_on(t, totals)

        @pl.when(t == 1)
        def _():
            pass_on(early, 0)
            pass_on(early, 1)

        return carry

    lax.fori_loop(0, early, other_step, 0)

    def step(t, carry):
        @pl.when(t > early)
        def _():
            pass_on(t, 1)

        prepare(t)
        tiles(0)
        tiles(rows)
        receive(t + 1, 0)

        @pl.when(t < nz - 2)
        def _():
            forward(t + 1, 0)

        hand_on(t, [query_part(r, 0, 2 * rows) for r in range(2)])
        return carry

    lax.fori_loop(early, nz - 1, step, 0)
    last = nz - 1
    receive(last, 1)
    prepare(last)
    tiles(rows)
    part_copies = []
    for m, total in enumerate((key_sum, value_sum)):
        part_send[m, :, :] = total[rows:, :].astype(BF16)
        copy = remote(
            part_send.at[m], part_recv.at[m], part_sems.at[0, m], part_sems.at[1, m], partner
        )
        copy.start()
        part_copies.append(copy)
    tiles(0)
    hand_on(last, [query_part(r, 0, 2 * rows) for r in range(2)])
    for load in loads[7:]:
        load.wait()
    started = list(part_copies)

    for r in range(2):
        trail_copy(r, nz - 1).wait_recv()
        lanes = slice(r * half, (r + 1) * half)
        low = (early_query[r, 0, :, :] + trail_recv[r, nz, :, :].astype(F32)).astype(BF16)
        flipped_ref[0:COLS, lanes] = low
        grads_ref[lanes, 0:COLS] = jnp.transpose(low.astype(F32)).astype(BF16)

    def reach(length, i):
        return (length - i) // 2

    def at(r, distance, position, length):
        return lax.rem(position + distance if r == 0 else position + length - distance, length)

    def half_of(r, i):
        return (i + r) % 2

    kinds = (
        (slice(0, COLS), zq_send, zq_recv),
        (slice(COLS, 3 * COLS), zk_send, zk_recv),
    )

    def weight_term(kind, z_at, side_at):
        first = pl.multiple_of((z_at * 2 + side_at) * COLS, COLS)
        return dot(flipped_ref[kinds[kind][0], :], input_ref[:, pl.ds(first, COLS)])

    z_copies = {}

    def z_message(kind, i):
        _, send, recv = kinds[kind]
        for r in range(2):
            total = weight_term(kind, at(r, reach(nz, i), z, nz), half_of(r, i))
            if i >= 2:
                z_copies[kind, r, i - 2].wait_recv()
                total = total + recv[r, i - 2, :, :].astype(F32)
            send[r, i, :, :] = total.astype(BF16)
            copy = remote(
                send.at[r, i],
                recv.at[r, i],
                z_sems.at[kind, 0, r, i],
                z_sems.at[kind, 1, r, i],
                z_ahead[r],
            )
            copy.start()
            z_copies[kind, r, i] = copy
            started.append(copy)

    yh_copies = {}

    def z_final(kind):
        rows_of, _, recv = kinds[kind]
        sides = []
        for side_at in range(2):
            total = weight_term(kind, z, side_at)
            for r in range(2):
                i = nz - 2 if half_of(r, nz - 2) == side_at else nz - 3
                z_copies[kind, r, i].wait_recv()
                total = total + recv[r, i, :, :].astype(F32)
            sides.append(total)
        yh_send[rows_of, :] = jnp.where(side == 0, sides[1], sides[0]).astype(BF16)
        copy = remote(
            yh_send.at[rows_of],
            yh_recv.at[rows_of],
            yh_sems.at[0, kind],
            yh_sems.at[1, kind],
            partner,
        )
        copy.start()
        yh_copies[kind] = copy
        started.append(copy)
        return jnp.where(side == 0, sides[0], sides[1])

    def weight_done(kind, kept):
        rows_of, _, _ = kinds[kind]
        yh_copies[kind].wait_recv()
        total = kept + yh_recv[rows_of, :].astype(F32)
        for place in range(total.shape[0] // COLS):
            m = rows_of.start // COLS + place
            weight_out[m, :, :] = jnp.transpose(total[place * COLS : (place + 1) * COLS, :])

    def input_term(x_at, y_at, core_at):
        first = pl.multiple_of(((y_at * nx + x_at) * 2 + core_at) * COLS, COLS)
        weights = jnp.concatenate(
            [weight_ref[m, pl.ds(first, COLS), :] for m in range(3)], axis=1
        )
        return dot_nt(grads_ref[...], weights)

    core_order = [(r, i) for i in range(nx - 1) for r in range(2)] + [(0, nx - 1), (0, nx)]
    core_copies = {}

    def core_message(place):
        r, i = core_order[place]
        term = input_term(at(r, reach(nx, i), x, nx), half_of(r, i), 1 - core)
        core_send[place, :, :] = term.astype(BF16)
        copy = remote(
            core_send.at[place],
            core_recv.at[place],
            core_sems.at[0, place],
            core_sems.at[1, place],
            twin,
        )
        copy.start()
        core_copies[r, i] = (place, copy)
        started.append(copy)

    x_copies = {}

    def input_pair(r, i):
        place, copy = core_copies[r, i]
        total = input_term(at(r, reach(nx, i), x, nx), half_of(r, i), core)
        copy.wait_recv()
        return total + core_recv[place, :, :].astype(F32)

    def x_message(i):
        for r in range(2):
            total = input_pair(r, i)
            if i >= 2:
                x_copies[r, i - 2].wait_recv()
                total = total + x_recv[r, i - 2, :, :].astype(F32)
            x_send[r, i, :, :] = total.astype(BF16)
            copy = remote(
                x_send.at[r, i], x_recv.at[r, i], x_sems.at[0, r, i], x_sems.at[1, r, i], x_ahead[r]
            )
            copy.start()
            x_copies[r, i] = copy
            started.append(copy)

    def x_final(place):
        total = input_pair(0, nx - 1 + place)
        y_at = half_of(0, nx - 1 + place)
        for r in range(2):
            i = nx - 2 if half_of(r, nx - 2) == y_at else nx - 3
            x_copies[r, i].wait_recv()
            total = total + x_recv[r, i, :, :].astype(F32)
        return y_at, total

    z_message(0, 0)
    z_message(0, 1)
    for m, total in ((1, key_sum), (2, value_sum)):
        part_copies[m - 1].wait_recv()
        low = (total[0:rows, :] + part_recv[m - 1, :, :].astype(F32)).astype(BF16)
        grads_ref[:, m * COLS : (m + 1) * COLS] = low
        flipped_ref[m * COLS : (m + 1) * COLS, :] = jnp.transpose(low.astype(F32)).astype(BF16)
    z_message(1, 0)
    for place in range(4):
        core_message(place)
    z_message(1, 1)
    z_message(0, 2)
    x_message(0)
    for place in range(4, 2 * nx):
        core_message(place)
    x_message(1)
    z_message(0, 3)
    z_message(1, 2)
    z_message(0, 4)
    z_message(1, 3)
    z_message(0, 5)
    x_message(2)
    z_message(1, 4)
    z_message(0, 6)
    finals = dict(x_final(place) for place in range(2))
    y_send[...] = jnp.where(low_side == 0, finals[1], finals[0]).astype(BF16)
    y_copy = remote(y_send, y_recv, y_sems.at[0], y_sems.at[1], neighbour)
    y_copy.start()
    mine = jnp.where(low_side == 0, finals[0], finals[1])
    z_message(1, 5)
    kept_query = z_final(0)
    z_message(1, 6)
    kept_key = z_final(1)
    y_copy.wait_recv()
    input_out[...] = (mine + y_recv[...].astype(F32)).astype(BF16)
    weight_done(0, kept_query)
    weight_done(1, kept_key)
    y_copy.wait_send()
    for copy in started:
        copy.wait_send()
    for r in range(2):

        def drain(t, carry, r=r):
            slot_copy(r, t, 0).wait_send()
            slot_copy(r, t, 1).wait_send()
            trail_copy(r, t + 1).wait_send()
            return carry

        lax.fori_loop(0, nz - 1, drain, 0)


def local(
    nz,
    nx,
    layer_input,
    qkv_weight,
    queries,
    key_states,
    value_states,
    attn_out,
    grad_out,
    log_sum_exp,
    frames,
):
    rows = queries.shape[0]
    half = rows // 2
    wide = 3 * COLS
    vmem = pl.BlockSpec(memory_space=pltpu.VMEM)
    anywhere = pl.BlockSpec(memory_space=pl.ANY)
    dma = pltpu.SemaphoreType.DMA
    stat = log_sum_exp.T

    def low(*shape):
        return pltpu.VMEM(shape, BF16)

    def full(*shape):
        return pltpu.VMEM(shape, F32)

    return pl.pallas_call(
        functools.partial(backward_kernel, nz, nx),
        out_shape=(
            jax.ShapeDtypeStruct((rows, COLS), BF16),
            jax.ShapeDtypeStruct((3, COLS, COLS), F32),
        ),
        in_specs=[anywhere] * 9,
        out_specs=(vmem, vmem),
        scratch_shapes=[
            pltpu.SMEM(frames.shape, jnp.int32),
            full(*stat.shape),
            low(rows, COLS),
            low(rows, COLS),
            low(rows, COLS),
            low(rows, COLS),
            low(rows, COLS),
            low(*layer_input.shape),
            low(*qkv_weight.shape),
            low(rows, COLS),
            low(rows, COLS),
            low(2, nz, 2 * COLS + 16, half),
            low(2, nz, COLS, half),
            low(2, nz + 1, COLS, half),
            low(2, 2 * rows, COLS),
            low(2, 2 * rows, COLS),
            low(COLS, 2 * rows),
            low(2, 4, COLS, half),
            low(2, 2, COLS, 2 * half),
            low(2, 2, 2 * rows, half),
            full(2 * rows, COLS),
            full(2 * rows, COLS),
            full(2, 3, COLS, half),
            low(2, rows, COLS),
            low(2, rows, COLS),
            low(rows, wide),
            low(wide, rows),
            low(2 * nx, rows, COLS),
            low(2 * nx, rows, COLS),
            low(2, nx - 1, rows, COLS),
            low(2, nx - 1, rows, COLS),
            low(rows, COLS),
            low(rows, COLS),
            low(2, nz - 1, COLS, COLS),
            low(2, nz - 1, COLS, COLS),
            low(2, nz - 1, 2 * COLS, COLS),
            low(2, nz - 1, 2 * COLS, COLS),
            low(wide, COLS),
            low(wide, COLS),
            dma((9,)),
            dma((2, 2, 2, nz)),
            dma((2, 2, nz + 1)),
            dma((2, 2)),
            dma((2, 2)),
            dma((2, 2 * nx)),
            dma((2, 2, nx - 1)),
            dma((2,)),
            dma((2, 2, 2, nz - 1)),
            dma((2, 2)),
        ],
        compiler_params=pltpu.CompilerParams(
            collective_id=0, has_side_effects=True, vmem_limit_bytes=56 * 2**20
        ),
        name="attention_backward",
    )(
        frames,
        stat,
        queries,
        key_states,
        value_states,
        attn_out,
        grad_out,
        layer_input,
        qkv_weight,
    )


def solution(mesh):
    nz = mesh.shape["seq"] // 2
    nx = mesh.shape["head"] // 4
    placed = (
        P("seq", None),
        P(None, None, "head"),
        P("seq", "head"),
        P("seq", "head"),
        P("seq", "head"),
        P("seq", "head"),
        P("seq", "head"),
        P("seq", "head"),
        P(),
    )
    return jax.shard_map(
        functools.partial(local, nz, nx),
        mesh=mesh,
        in_specs=placed,
        out_specs=(P("seq", "head"), P(None, "seq", "head")),
        check_vma=False,
    )
```

```python
import functools

import jax
import jax.numpy as jnp
from jax import lax
from jax.experimental import pallas as pl
from jax.experimental.pallas import tpu as pltpu
from jax.sharding import PartitionSpec as P

BLOCK = 64
HEAD_SIZE = 64
COLS = 2 * HEAD_SIZE
FRAMES = 32
CHUNK = 256
HIDDEN = -16384.0
LOG2E = 1.4426950408889634
MESH = pl.DeviceIdType.MESH
PIECES = (0, 128, 272)
BF16 = jnp.bfloat16
F32 = jnp.float32


def dot(left, right):
    return jnp.dot(left, right, preferred_element_type=F32)


def dot_nt(left, right):
    return lax.dot_general(left, right, (((1,), (1,)), ((), ())), preferred_element_type=F32)


def greet(peers):
    barrier = pltpu.get_barrier_semaphore()
    for peer in peers:
        pl.semaphore_signal(barrier, inc=1, device_id=peer, device_id_type=MESH)
    pl.semaphore_wait(barrier, len(peers))


def remote(source, target, send_sem, recv_sem, peer):
    return pltpu.make_async_remote_copy(
        src_ref=source,
        dst_ref=target,
        send_sem=send_sem,
        recv_sem=recv_sem,
        device_id=peer,
        device_id_type=MESH,
    )


def backward_kernel(
    nz,
    nx,
    frames_hbm,
    stat_hbm,
    query_hbm,
    key_hbm,
    value_hbm,
    out_hbm,
    grad_hbm,
    input_hbm,
    weight_hbm,
    input_out,
    weight_out,
    frames_ref,
    stat_ref,
    query_ref,
    key_ref,
    value_ref,
    out_ref,
    grad_ref,
    input_ref,
    weight_ref,
    key_other,
    value_other,
    slots,
    trail_send,
    trail_recv,
    key_wide,
    value_wide,
    key_flip,
    fixed,
    paired,
    score_low,
    key_sum,
    value_sum,
    early_query,
    part_send,
    part_recv,
    grads_ref,
    flipped_ref,
    core_send,
    core_recv,
    x_send,
    x_recv,
    x_term,
    own_term,
    y_send,
    y_recv,
    zq_term,
    zq_send,
    zq_recv,
    zq_last,
    zk_term,
    zk_send,
    zk_recv,
    zk_last,
    near_term,
    near_send,
    near_recv,
    load_sems,
    slot_sems,
    trail_sems,
    pair_sems,
    part_sems,
    core_sems,
    x_sems,
    y_sems,
    z_sems,
    last_sems,
    near_sems,
):
    loads = [
        pltpu.make_async_copy(source, target, load_sems.at[i])
        for i, (source, target) in enumerate(
            (
                (grad_hbm, grad_ref),
                (query_hbm, query_ref),
                (out_hbm, out_ref),
                (stat_hbm, stat_ref),
                (key_hbm, key_ref),
                (value_hbm, value_ref),
                (frames_hbm, frames_ref),
                (input_hbm, input_ref),
                (weight_hbm, weight_ref),
            )
        )
    ]
    for load in loads:
        load.start()

    rows = query_ref.shape[0]
    half = rows // 2
    blocks = rows // BLOCK
    count = 2 * nz
    seq = lax.axis_index("seq")
    head = lax.axis_index("head")
    side = lax.rem(seq, 2)
    z = seq // 2
    partner_seq = seq + 1 - 2 * side
    partner = {"seq": partner_seq}
    z_ahead = ({"seq": lax.rem(seq + 2, count)}, {"seq": lax.rem(seq + count - 2, count)})
    core = lax.rem(head, 2)
    x = lax.rem(head // 2, nx)
    low_side = head // (2 * nx)
    twin = {"head": head + 1 - 2 * core}
    plane = low_side * 2 * nx + core
    x_ahead = (
        {"head": plane + 2 * lax.rem(x + 1, nx)},
        {"head": plane + 2 * lax.rem(x + nx - 1, nx)},
    )
    neighbour = {"head": (1 - low_side) * 2 * nx + 2 * x + core}
    slants = [{"seq": 2 * lax.rem(z + dz, nz) + 1 - side} for dz in (1, nz - 1)]
    greet((partner, *z_ahead, *slants, twin, neighbour, *x_ahead))

    pair_copies = [
        remote(key_hbm, key_other, pair_sems.at[0, 0], pair_sems.at[1, 0], partner),
        remote(value_hbm, value_other, pair_sems.at[0, 1], pair_sems.at[1, 1], partner),
    ]
    for copy in pair_copies:
        copy.start()

    def slot_copy(r, t, part):
        here = pl.ds(PIECES[part], PIECES[part + 1] - PIECES[part])
        return remote(
            slots.at[r, t, here],
            slots.at[r, t + 1, here],
            slot_sems.at[0, part, r, t],
            slot_sems.at[1, part, r, t + 1],
            z_ahead[r],
        )

    def trail_copy(r, t):
        return remote(
            trail_send.at[r, t],
            trail_recv.at[r, t + 1],
            trail_sems.at[0, r, t],
            trail_sems.at[1, r, t + 1],
            z_ahead[r],
        )

    for load in loads[:4]:
        load.wait()
    grad_wide = grad_ref[...].astype(F32)
    query_flip = jnp.transpose(query_ref[...].astype(F32) * (HEAD_SIZE**-0.5))
    grad_flip = jnp.transpose(grad_wide)
    delta_flip = jnp.transpose(grad_wide * out_ref[...].astype(F32))
    aux_row = lax.broadcasted_iota(jnp.int32, (16, rows), 0)
    aux = jnp.zeros((16, rows), F32)
    for h in range(2):
        delta = jnp.sum(
            delta_flip[h * HEAD_SIZE : (h + 1) * HEAD_SIZE, :], axis=0, keepdims=True
        )
        for first, value in ((3 * h, stat_ref[h : h + 1, :]), (6 + 3 * h, delta)):
            rest = value
            for place in range(3):
                piece = rest.astype(BF16).astype(F32)
                aux = jnp.where(aux_row == first + place, piece, aux)
                rest = rest - piece
    for r in range(2):
        lanes = slice(r * half, (r + 1) * half)
        slots[r, 0, 0:COLS, :] = query_flip[:, lanes].astype(BF16)
        slots[r, 0, COLS : 2 * COLS, :] = grad_flip[:, lanes].astype(BF16)
        slots[r, 0, 2 * COLS : 2 * COLS + 16, :] = aux[:, lanes].astype(BF16)

    lane = lax.broadcasted_iota(jnp.int32, (BLOCK, COLS), 1)
    inner = lax.rem(lane, HEAD_SIZE)

    def build_keys(keys_from, values_from, base, owner):
        for b in range(blocks):
            here = slice(b * BLOCK, (b + 1) * BLOCK)
            there = slice(base + b * BLOCK, base + (b + 1) * BLOCK)
            frame = frames_ref[owner * blocks + b]
            keys = keys_from[here, :].astype(F32)
            values = values_from[here, :].astype(F32)
            for h in range(2):
                mine = (lane >= h * HEAD_SIZE) & (lane < (h + 1) * HEAD_SIZE)
                stat_at = (inner >= FRAMES + 3 * h) & (inner < FRAMES + 3 * h + 3)
                delta_at = (inner >= FRAMES + 6 + 3 * h) & (inner < FRAMES + 9 + 3 * h)
                key_more = jnp.where(inner == frame, 1.0, jnp.where(stat_at, -1.0, 0.0))
                value_more = jnp.where(delta_at, -1.0, 0.0)
                key_wide[h, there, :] = jnp.where(mine, keys, key_more).astype(BF16)
                value_wide[h, there, :] = jnp.where(mine, values, value_more).astype(BF16)
        key_flip[:, base : base + rows] = jnp.transpose(
            keys_from[...].astype(F32) * (HEAD_SIZE**-0.5)
        ).astype(BF16)

    frame_row = lax.broadcasted_iota(jnp.int32, (FRAMES, half), 0)
    frame_lane = lax.broadcasted_iota(jnp.int32, (FRAMES, half), 1)

    def prepare(t):
        for r, owner in enumerate((lax.rem(seq + 2 * (nz - t), count), lax.rem(seq + 2 * t, count))):
            first = owner * blocks + r * (blocks // 2)
            seen = jnp.full((FRAMES, half), frames_ref[first + blocks // 2 - 1], jnp.int32)
            for i in range(blocks // 2 - 2, -1, -1):
                seen = jnp.where(frame_lane < (i + 1) * BLOCK, frames_ref[first + i], seen)
            hidden = jnp.where(frame_row > seen, HIDDEN, 0.0).astype(BF16)
            extra = jnp.concatenate(
                [hidden, slots[r, t, 2 * COLS : 2 * COLS + 16, :], jnp.zeros((16, half), BF16)],
                axis=0,
            )
            zero = jnp.zeros((HEAD_SIZE, half), BF16)
            for which in range(2):
                low = slots[r, t, which * COLS : which * COLS + HEAD_SIZE, :]
                high = slots[r, t, which * COLS + HEAD_SIZE : (which + 1) * COLS, :]
                fixed[r, 2 * which, :, :] = jnp.concatenate([low, extra], axis=0)
                fixed[r, 2 * which + 1, :, :] = jnp.concatenate([extra, high], axis=0)
                paired[r, which, :, :] = jnp.concatenate(
                    [
                        jnp.concatenate([low, zero], axis=1),
                        jnp.concatenate([zero, high], axis=1),
                    ],
                    axis=0,
                )

    def tile(r, start):
        here = pl.ds(start, CHUNK)
        probs, scores = [], []
        for h in range(2):
            score = dot(key_wide[h, here, :], fixed[r, h, :, :])
            prob = jnp.exp2(score * LOG2E)
            prob_grad = dot(value_wide[h, here, :], fixed[r, 2 + h, :, :])
            score_grad = (prob * prob_grad).astype(BF16)
            score_low[r, h, here, :] = score_grad
            probs.append(prob.astype(BF16))
            scores.append(score_grad)
        value_sum[here, :] += dot_nt(jnp.concatenate(probs, axis=1), paired[r, 1, :, :])
        key_sum[here, :] += dot_nt(jnp.concatenate(scores, axis=1), paired[r, 0, :, :])

    def tiles(first):
        for c in range(rows // CHUNK):
            for r in range(2):
                tile(r, first + c * CHUNK)

    def query_part(r, first, length):
        return jnp.concatenate(
            [
                dot(
                    key_flip[h * HEAD_SIZE : (h + 1) * HEAD_SIZE, first : first + length],
                    score_low[r, h, first : first + length, :],
                )
                for h in range(2)
            ],
            axis=0,
        )

    every = range(len(PIECES) - 1)

    def forward(t, part):
        for r in range(2):
            slot_copy(r, t, part).start()

    def pass_on(t, parts):
        for part in parts:
            for r in range(2):
                slot_copy(r, t - 1, part).wait_recv()

            if isinstance(t, int):
                continue

            @pl.when(t < nz - 1)
            def _(part=part):
                forward(t, part)

    def hand_on(t, totals):
        @pl.when(t > 1)
        def _():
            for r in range(2):
                trail_copy(r, t - 1).wait_recv()

        for r in range(2):
            total = totals[r] + trail_recv[r, t, :, :].astype(F32)
            trail_send[r, t, :, :] = total.astype(BF16)
            trail_copy(r, t).start()

    early = min(2, nz - 1)
    for part in every:
        forward(0, part)
    for load in loads[4:7]:
        load.wait()
    build_keys(key_ref, value_ref, 0, seq)
    key_sum[...] = jnp.zeros_like(key_sum)
    value_sum[...] = jnp.zeros_like(value_sum)
    for r in range(2):
        trail_recv[r, 1, :, :] = jnp.zeros((COLS, half), BF16)

    def own_step(t, carry):
        @pl.when(t > 0)
        def _():
            pass_on(t, every)

        prepare(t)
        tiles(0)
        for r in range(2):
            early_query[r, t, :, :] = query_part(r, 0, rows)
        return carry

    lax.fori_loop(0, early, own_step, 0)
    for copy in pair_copies:
        copy.wait()
    build_keys(key_other, value_other, rows, partner_seq)

    def other_step(t, carry):
        prepare(t)
        tiles(rows)
        totals = [early_query[r, t, :, :] + query_part(r, rows, rows) for r in range(2)]

        @pl.when(t == 0)
        def _():
            for r in range(2):
                early_query[r, 0, :, :] = totals[r]

        @pl.when(t > 0)
        def _():
            hand_on(t, totals)

        @pl.when(t == 0)
        def _():
            pass_on(t + early - 0, every)

        return carry

    lax.fori_loop(0, early, other_step, 0)

    def step(t, carry):
        @pl.when(t > early)
        def _():
            pass_on(t, every[1:])

        prepare(t)
        tiles(0)
        tiles(rows)
        pass_on(t + 1, every[:1])
        hand_on(t, [query_part(r, 0, 2 * rows) for r in range(2)])
        return carry

    lax.fori_loop(early, nz - 1, step, 0)
    last = nz - 1
    for load in loads[7:]:
        load.wait()
    pass_on(last, every[1:])
    prepare(last)
    tiles(rows)
    part_copies = []
    for m, total in enumerate((key_sum, value_sum)):
        part_send[m, :, :] = total[rows:, :].astype(BF16)
        copy = remote(
            part_send.at[m], part_recv.at[m], part_sems.at[0, m], part_sems.at[1, m], partner
        )
        copy.start()
        part_copies.append(copy)
    tiles(0)
    hand_on(last, [query_part(r, 0, 2 * rows) for r in range(2)])
    started = list(part_copies)

    for r in range(2):
        trail_copy(r, nz - 1).wait_recv()
        lanes = slice(r * half, (r + 1) * half)
        low = (early_query[r, 0, :, :] + trail_recv[r, nz, :, :].astype(F32)).astype(BF16)
        flipped_ref[0:COLS, lanes] = low
        grads_ref[lanes, 0:COLS] = jnp.transpose(low.astype(F32)).astype(BF16)

    def launch(copy):
        copy.start()
        started.append(copy)
        return copy

    def at(r, distance):
        return lax.rem(z + distance if r == 0 else z + nz - distance, nz)

    def half_of(r, i):
        return (i + r) % 2

    kinds = (
        (slice(0, COLS), zq_term, zq_send, zq_recv, zq_last),
        (slice(COLS, 3 * COLS), zk_term, zk_send, zk_recv, zk_last),
    )
    z_copies = {}

    def weight_term(kind, z_at, side_at):
        first = pl.multiple_of((z_at * 2 + side_at) * COLS, COLS)
        return dot(flipped_ref[kinds[kind][0], :], input_ref[:, pl.ds(first, COLS)])

    def z_term(kind, i):
        for r in range(2):
            kinds[kind][1][r, i, :, :] = weight_term(kind, at(r, (nz - i) // 2), half_of(r, i))

    def z_message(kind, i, ready=False):
        _, term, send, recv, final = kinds[kind]
        if not ready:
            z_term(kind, i)
        for r in range(2):
            total = term[r, i, :, :]
            if i >= 2:
                z_copies[kind, r, i - 2].wait_recv()
                total = total + recv[r, i - 2, :, :].astype(F32)
            send[r, i, :, :] = total.astype(BF16)
            if i < nz - 3:
                copy = remote(
                    send.at[r, i],
                    recv.at[r, i],
                    z_sems.at[kind, 0, r, i],
                    z_sems.at[kind, 1, r, i],
                    z_ahead[r],
                )
            else:
                copy = remote(
                    send.at[r, i],
                    final.at[r, side],
                    z_sems.at[kind, 0, r, i],
                    last_sems.at[kind, r, side],
                    {"seq": 2 * at(r, 1) + half_of(r, i)},
                )
            z_copies[kind, r, i] = launch(copy)

    near_copies = {}

    def z_near(kind):
        rows_of = kinds[kind][0]
        near_send[rows_of, :] = weight_term(kind, z, 1 - side).astype(BF16)
        near_copies[kind] = launch(
            remote(
                near_send.at[rows_of],
                near_recv.at[rows_of],
                near_sems.at[0, kind],
                near_sems.at[1, kind],
                partner,
            )
        )
        near_term[rows_of, :] = weight_term(kind, z, side)

    def z_final(kind):
        rows_of, _, send, _, final = kinds[kind]
        near_copies[kind].wait_recv()
        total = near_term[rows_of, :] + near_recv[rows_of, :].astype(F32)
        for r in range(2):
            for source in range(2):
                remote(
                    send.at[r, 0],
                    final.at[r, source],
                    z_sems.at[kind, 0, r, 0],
                    last_sems.at[kind, r, source],
                    partner,
                ).wait_recv()
                total = total + final[r, source, :, :].astype(F32)
        for place in range(total.shape[0] // COLS):
            m = rows_of.start // COLS + place
            weight_out[m, :, :] = jnp.transpose(total[place * COLS : (place + 1) * COLS, :])

    def input_term(dx, core_at):
        weights = []
        for y_at in range(2):
            first = pl.multiple_of(((y_at * nx + lax.rem(x + dx, nx)) * 2 + core_at) * COLS, COLS)
            weights.append(
                jnp.concatenate([weight_ref[m, pl.ds(first, COLS), :] for m in range(3)], axis=1)
            )
        return dot_nt(grads_ref[...], jnp.concatenate(weights, axis=0))

    core_copies = {}

    def core_message(dx):
        core_send[dx, :, :] = input_term(dx, 1 - core).astype(BF16)
        core_copies[dx] = launch(
            remote(
                core_send.at[dx],
                core_recv.at[dx],
                core_sems.at[0, dx],
                core_sems.at[1, dx],
                twin,
            )
        )

    x_copies = {}

    def x_message(r, i):
        if i >= 2:
            x_copies[r, i - 2].wait_recv()
            total = x_term[r, :, :] + x_recv[r, i - 2, :, :].astype(F32)
            x_send[r, i, :, :] = total.astype(BF16)
        x_copies[r, i] = launch(
            remote(
                x_send.at[r, i], x_recv.at[r, i], x_sems.at[0, r, i], x_sems.at[1, r, i], x_ahead[r]
            )
        )

    def input_pair(dx):
        total = input_term(dx, core)
        core_copies[dx].wait_recv()
        total = total + core_recv[dx, :, :].astype(F32)
        return [total[:, y_at * COLS : (y_at + 1) * COLS] for y_at in range(2)]

    def x_first():
        sides = input_pair(2)
        for r in range(2):
            x_send[r, 0, :, :] = sides[r].astype(BF16)
            x_message(r, 0)

    def x_second(r):
        sides = input_pair(1 if r == 0 else nx - 1)
        x_send[r, 1, :, :] = sides[1 - r].astype(BF16)
        x_message(r, 1)
        x_term[r, :, :] = sides[r]

    def x_own():
        for y_at, total in enumerate(input_pair(0)):
            own_term[y_at, :, :] = total

    def x_final():
        totals = []
        for y_at in range(2):
            total = own_term[y_at, :, :]
            for r in range(2):
                i = 2 if r == y_at else 1
                x_copies[r, i].wait_recv()
                total = total + x_recv[r, i, :, :].astype(F32)
            totals.append(total)
        y_send[...] = jnp.where(low_side == 0, totals[1], totals[0]).astype(BF16)
        own_term[0, :, :] = jnp.where(low_side == 0, totals[0], totals[1])
        return launch(remote(y_send, y_recv, y_sems.at[0], y_sems.at[1], neighbour))

    def drain(t, carry):
        for r in range(2):
            for part in every:
                slot_copy(r, t, part).wait_send()
            trail_copy(r, t + 1).wait_send()
        return carry

    z_message(0, 0)
    z_message(0, 1)
    z_near(0)
    for i in range(2, nz - 1):
        z_term(0, i)
    lax.fori_loop(0, nz - 1, drain, 0)
    for m, total in ((1, key_sum), (2, value_sum)):
        part_copies[m - 1].wait_recv()
        low = (total[0:rows, :] + part_recv[m - 1, :, :].astype(F32)).astype(BF16)
        grads_ref[:, m * COLS : (m + 1) * COLS] = low
        flipped_ref[m * COLS : (m + 1) * COLS, :] = jnp.transpose(low.astype(F32)).astype(BF16)
    z_message(1, 0)
    core_message(2)
    z_message(1, 1)
    core_message(1)
    z_message(0, 2, True)
    z_message(0, 3, True)
    x_first()
    core_message(3)
    x_second(0)
    core_message(0)
    x_second(1)
    z_message(1, 2)
    z_message(1, 3)
    z_message(0, 4, True)
    z_message(0, 5, True)
    x_own()
    z_near(1)
    for i in range(4, nz - 1):
        z_term(1, i)
    x_message(0, 2)
    x_message(1, 2)
    z_message(1, 4, True)
    z_message(1, 5, True)
    z_message(0, 6, True)
    z_message(1, 6, True)
    z_final(0)
    y_copy = x_final()
    z_final(1)
    y_copy.wait_recv()
    input_out[...] = (own_term[0, :, :] + y_recv[...].astype(F32)).astype(BF16)
    for copy in started:
        copy.wait_send()


def local(
    nz,
    nx,
    layer_input,
    qkv_weight,
    queries,
    key_states,
    value_states,
    attn_out,
    grad_out,
    log_sum_exp,
    frames,
):
    rows = queries.shape[0]
    half = rows // 2
    wide = 3 * COLS
    vmem = pl.BlockSpec(memory_space=pltpu.VMEM)
    anywhere = pl.BlockSpec(memory_space=pltpu.HBM)
    dma = pltpu.SemaphoreType.DMA
    stat = log_sum_exp.T

    def low(*shape):
        return pltpu.VMEM(shape, BF16)

    def full(*shape):
        return pltpu.VMEM(shape, F32)

    return pl.pallas_call(
        functools.partial(backward_kernel, nz, nx),
        out_shape=(
            pltpu.VMEM((rows, COLS), BF16),
            pltpu.VMEM((3, COLS, COLS), F32),
        ),
        in_specs=[anywhere] * 9,
        out_specs=(vmem, vmem),
        scratch_shapes=[
            pltpu.SMEM(frames.shape, jnp.int32),
            full(*stat.shape),
            low(rows, COLS),
            low(rows, COLS),
            low(rows, COLS),
            low(rows, COLS),
            low(rows, COLS),
            low(*layer_input.shape),
            low(*qkv_weight.shape),
            low(rows, COLS),
            low(rows, COLS),
            low(2, nz, 2 * COLS + 16, half),
            low(2, nz, COLS, half),
            low(2, nz + 1, COLS, half),
            low(2, 2 * rows, COLS),
            low(2, 2 * rows, COLS),
            low(COLS, 2 * rows),
            low(2, 4, COLS, half),
            low(2, 2, COLS, 2 * half),
            low(2, 2, 2 * rows, half),
            full(2 * rows, COLS),
            full(2 * rows, COLS),
            full(2, 2, COLS, half),
            low(2, rows, COLS),
            low(2, rows, COLS),
            low(rows, wide),
            low(wide, rows),
            low(nx, rows, 2 * COLS),
            low(nx, rows, 2 * COLS),
            low(2, 3, rows, COLS),
            low(2, 3, rows, COLS),
            full(2, rows, COLS),
            full(2, rows, COLS),
            low(rows, COLS),
            low(rows, COLS),
            full(2, nz - 1, COLS, COLS),
            low(2, nz - 1, COLS, COLS),
            low(2, nz - 3, COLS, COLS),
            low(2, 2, COLS, COLS),
            full(2, nz - 1, 2 * COLS, COLS),
            low(2, nz - 1, 2 * COLS, COLS),
            low(2, nz - 3, 2 * COLS, COLS),
            low(2, 2, 2 * COLS, COLS),
            full(wide, COLS),
            low(wide, COLS),
            low(wide, COLS),
            dma((9,)),
            dma((2, len(PIECES) - 1, 2, nz)),
            dma((2, 2, nz + 1)),
            dma((2, 2)),
            dma((2, 2)),
            dma((2, nx)),
            dma((2, 2, 3)),
            dma((2,)),
            dma((2, 2, 2, nz - 1)),
            dma((2, 2, 2)),
            dma((2, 2)),
        ],
        compiler_params=pltpu.CompilerParams(
            collective_id=0, has_side_effects=True, vmem_limit_bytes=48 * 2**20
        ),
        name="attention_backward",
    )(
        *(
            pltpu.with_memory_space_constraint(array, pltpu.HBM)
            for array in (
                frames,
                stat,
                queries,
                key_states,
                value_states,
                attn_out,
                grad_out,
                layer_input,
                qkv_weight,
            )
        )
    )


def solution(mesh):
    nz = mesh.shape["seq"] // 2
    nx = mesh.shape["head"] // 4
    placed = (
        P("seq", None),
        P(None, None, "head"),
        P("seq", "head"),
        P("seq", "head"),
        P("seq", "head"),
        P("seq", "head"),
        P("seq", "head"),
        P("seq", "head"),
        P(),
    )
    return jax.shard_map(
        functools.partial(local, nz, nx),
        mesh=mesh,
        in_specs=placed,
        out_specs=(P("seq", "head"), P(None, "seq", "head")),
        check_vma=False,
    )
```

```python
import functools

import jax
import jax.numpy as jnp
from jax import lax
from jax.experimental import pallas as pl
from jax.experimental.pallas import tpu as pltpu
from jax.sharding import PartitionSpec as P

BLOCK = 64
HEAD_SIZE = 64
COLS = 2 * HEAD_SIZE
FRAMES = 32
CHUNK = 256
HIDDEN = -16384.0
LOG2E = 1.4426950408889634
MESH = pl.DeviceIdType.MESH
PIECES = (0, 128, 272)
BF16 = jnp.bfloat16
F32 = jnp.float32


def dot(left, right):
    return jnp.dot(left, right, preferred_element_type=F32)


def dot_nt(left, right):
    return lax.dot_general(left, right, (((1,), (1,)), ((), ())), preferred_element_type=F32)


def greet(peers):
    barrier = pltpu.get_barrier_semaphore()
    for peer in peers:
        pl.semaphore_signal(barrier, inc=1, device_id=peer, device_id_type=MESH)


def remote(source, target, send_sem, recv_sem, peer):
    return pltpu.make_async_remote_copy(
        src_ref=source,
        dst_ref=target,
        send_sem=send_sem,
        recv_sem=recv_sem,
        device_id=peer,
        device_id_type=MESH,
    )


def backward_kernel(
    nz,
    nx,
    frames_hbm,
    stat_hbm,
    query_hbm,
    key_hbm,
    value_hbm,
    out_hbm,
    grad_hbm,
    input_hbm,
    weight_hbm,
    input_out,
    weight_out,
    frames_ref,
    stat_ref,
    query_ref,
    key_ref,
    value_ref,
    out_ref,
    grad_ref,
    input_ref,
    weight_ref,
    key_other,
    value_other,
    slots,
    trail_send,
    trail_recv,
    key_wide,
    value_wide,
    key_flip,
    fixed,
    paired,
    score_low,
    key_sum,
    value_sum,
    early_query,
    part_send,
    part_recv,
    grads_ref,
    flipped_ref,
    core_send,
    core_recv,
    xa_send,
    xa_recv,
    xa_term,
    xa_own,
    xb_send,
    xb_recv,
    yb_send,
    yb_recv,
    yb_term,
    ya_send,
    ya_recv,
    zq_term,
    zq_send,
    zq_recv,
    zq_last,
    zk_term,
    zk_send,
    zk_recv,
    zk_last,
    near_term,
    near_send,
    near_recv,
    load_sems,
    slot_sems,
    trail_sems,
    pair_sems,
    part_sems,
    core_sems,
    xa_sems,
    xb_sems,
    y_sems,
    z_sems,
    last_sems,
    near_sems,
):
    loads = [
        pltpu.make_async_copy(source, target, load_sems.at[i])
        for i, (source, target) in enumerate(
            (
                (query_hbm, query_ref),
                (grad_hbm, grad_ref),
                (out_hbm, out_ref),
                (stat_hbm, stat_ref),
                (key_hbm, key_ref),
                (value_hbm, value_ref),
                (frames_hbm, frames_ref),
                (input_hbm, input_ref),
                (weight_hbm, weight_ref),
            )
        )
    ]
    for load in loads:
        load.start()

    rows = query_ref.shape[0]
    half = rows // 2
    blocks = rows // BLOCK
    count = 2 * nz
    seq = lax.axis_index("seq")
    head = lax.axis_index("head")
    side = lax.rem(seq, 2)
    z = seq // 2
    partner_seq = seq + 1 - 2 * side
    partner = {"seq": partner_seq}
    z_ahead = ({"seq": lax.rem(seq + 2, count)}, {"seq": lax.rem(seq + count - 2, count)})
    core = lax.rem(head, 2)
    x = lax.rem(head // 2, nx)
    low_side = head // (2 * nx)
    twin = {"head": head + 1 - 2 * core}
    plane = low_side * 2 * nx + core
    x_ahead = (
        {"head": plane + 2 * lax.rem(x + 1, nx)},
        {"head": plane + 2 * lax.rem(x + nx - 1, nx)},
    )
    neighbour = {"head": (1 - low_side) * 2 * nx + 2 * x + core}
    slants = [{"seq": 2 * lax.rem(z + dz, nz) + 1 - side} for dz in (1, nz - 1)]
    peers = (*z_ahead, partner, *slants, twin, neighbour, *x_ahead)
    greet(peers)

    pair_copies = [
        remote(key_hbm, key_other, pair_sems.at[0, 0], pair_sems.at[1, 0], partner),
        remote(value_hbm, value_other, pair_sems.at[0, 1], pair_sems.at[1, 1], partner),
    ]
    def slot_copy(r, t, part):
        here = pl.ds(PIECES[part], PIECES[part + 1] - PIECES[part])
        return remote(
            slots.at[r, t, here],
            slots.at[r, t + 1, here],
            slot_sems.at[0, part, r, t],
            slot_sems.at[1, part, r, t + 1],
            z_ahead[r],
        )

    def trail_copy(r, t):
        return remote(
            trail_send.at[r, t],
            trail_recv.at[r, t + 1],
            trail_sems.at[0, r, t],
            trail_sems.at[1, r, t + 1],
            z_ahead[r],
        )

    every = range(len(PIECES) - 1)

    def forward(t, part):
        for r in range(2):
            slot_copy(r, t, part).start()

    loads[0].wait()
    query_flip = jnp.transpose(query_ref[...].astype(F32) * (HEAD_SIZE**-0.5))
    for r in range(2):
        slots[r, 0, 0:COLS, :] = query_flip[:, r * half : (r + 1) * half].astype(BF16)
    pl.semaphore_wait(pltpu.get_barrier_semaphore(), len(peers))
    for copy in pair_copies:
        copy.start()
    forward(0, 0)
    for load in loads[1:4]:
        load.wait()
    grad_wide = grad_ref[...].astype(F32)
    grad_flip = jnp.transpose(grad_wide)
    delta_flip = jnp.transpose(grad_wide * out_ref[...].astype(F32))
    aux_row = lax.broadcasted_iota(jnp.int32, (16, rows), 0)
    aux = jnp.zeros((16, rows), F32)
    for h in range(2):
        delta = jnp.sum(
            delta_flip[h * HEAD_SIZE : (h + 1) * HEAD_SIZE, :], axis=0, keepdims=True
        )
        for first, value in ((3 * h, stat_ref[h : h + 1, :]), (6 + 3 * h, delta)):
            rest = value
            for place in range(3):
                piece = rest.astype(BF16).astype(F32)
                aux = jnp.where(aux_row == first + place, piece, aux)
                rest = rest - piece
    for r in range(2):
        lanes = slice(r * half, (r + 1) * half)
        slots[r, 0, COLS : 2 * COLS, :] = grad_flip[:, lanes].astype(BF16)
        slots[r, 0, 2 * COLS : 2 * COLS + 16, :] = aux[:, lanes].astype(BF16)

    lane = lax.broadcasted_iota(jnp.int32, (BLOCK, COLS), 1)
    inner = lax.rem(lane, HEAD_SIZE)

    def build_keys(keys_from, values_from, base, owner):
        for b in range(blocks):
            here = slice(b * BLOCK, (b + 1) * BLOCK)
            there = slice(base + b * BLOCK, base + (b + 1) * BLOCK)
            frame = frames_ref[owner * blocks + b]
            keys = keys_from[here, :].astype(F32)
            values = values_from[here, :].astype(F32)
            for h in range(2):
                mine = (lane >= h * HEAD_SIZE) & (lane < (h + 1) * HEAD_SIZE)
                stat_at = (inner >= FRAMES + 3 * h) & (inner < FRAMES + 3 * h + 3)
                delta_at = (inner >= FRAMES + 6 + 3 * h) & (inner < FRAMES + 9 + 3 * h)
                key_more = jnp.where(inner == frame, 1.0, jnp.where(stat_at, -1.0, 0.0))
                value_more = jnp.where(delta_at, -1.0, 0.0)
                key_wide[h, there, :] = jnp.where(mine, keys, key_more).astype(BF16)
                value_wide[h, there, :] = jnp.where(mine, values, value_more).astype(BF16)
        key_flip[:, base : base + rows] = jnp.transpose(
            keys_from[...].astype(F32) * (HEAD_SIZE**-0.5)
        ).astype(BF16)

    frame_row = lax.broadcasted_iota(jnp.int32, (FRAMES, half), 0)
    frame_lane = lax.broadcasted_iota(jnp.int32, (FRAMES, half), 1)

    def prepare(t):
        for r, owner in enumerate((lax.rem(seq + 2 * (nz - t), count), lax.rem(seq + 2 * t, count))):
            first = owner * blocks + r * (blocks // 2)
            seen = jnp.full((FRAMES, half), frames_ref[first + blocks // 2 - 1], jnp.int32)
            for i in range(blocks // 2 - 2, -1, -1):
                seen = jnp.where(frame_lane < (i + 1) * BLOCK, frames_ref[first + i], seen)
            hidden = jnp.where(frame_row > seen, HIDDEN, 0.0).astype(BF16)
            extra = jnp.concatenate(
                [hidden, slots[r, t, 2 * COLS : 2 * COLS + 16, :], jnp.zeros((16, half), BF16)],
                axis=0,
            )
            zero = jnp.zeros((HEAD_SIZE, half), BF16)
            for which in range(2):
                low = slots[r, t, which * COLS : which * COLS + HEAD_SIZE, :]
                high = slots[r, t, which * COLS + HEAD_SIZE : (which + 1) * COLS, :]
                fixed[r, 2 * which, :, :] = jnp.concatenate([low, extra], axis=0)
                fixed[r, 2 * which + 1, :, :] = jnp.concatenate([extra, high], axis=0)
                paired[r, which, :, :] = jnp.concatenate(
                    [
                        jnp.concatenate([low, zero], axis=1),
                        jnp.concatenate([zero, high], axis=1),
                    ],
                    axis=0,
                )

    def tile(r, start):
        here = pl.ds(start, CHUNK)
        probs, scores = [], []
        for h in range(2):
            score = dot(key_wide[h, here, :], fixed[r, h, :, :])
            prob = jnp.exp2(score * LOG2E)
            prob_grad = dot(value_wide[h, here, :], fixed[r, 2 + h, :, :])
            score_grad = (prob * prob_grad).astype(BF16)
            score_low[r, h, here, :] = score_grad
            probs.append(prob.astype(BF16))
            scores.append(score_grad)
        value_sum[here, :] += dot_nt(jnp.concatenate(probs, axis=1), paired[r, 1, :, :])
        key_sum[here, :] += dot_nt(jnp.concatenate(scores, axis=1), paired[r, 0, :, :])

    def tiles(first):
        for c in range(rows // CHUNK):
            for r in range(2):
                tile(r, first + c * CHUNK)

    def query_part(r, first, length):
        return jnp.concatenate(
            [
                dot(
                    key_flip[h * HEAD_SIZE : (h + 1) * HEAD_SIZE, first : first + length],
                    score_low[r, h, first : first + length, :],
                )
                for h in range(2)
            ],
            axis=0,
        )

    def pass_on(t, parts, always=False):
        for part in parts:
            for r in range(2):
                slot_copy(r, t - 1, part).wait_recv()

            if isinstance(t, int):
                if always:
                    forward(t, part)
                continue

            @pl.when(t < nz - 1)
            def _(part=part):
                forward(t, part)

    def hand_on(t, totals):
        if not isinstance(t, int) or t > 1:
            for r in range(2):
                trail_copy(r, t - 1).wait_recv()

        for r in range(2):
            total = totals[r] + trail_recv[r, t, :, :].astype(F32)
            trail_send[r, t, :, :] = total.astype(BF16)
            trail_copy(r, t).start()

    early = min(2, nz - 1)
    forward(0, 1)
    for load in loads[4:7]:
        load.wait()
    build_keys(key_ref, value_ref, 0, seq)
    key_sum[...] = jnp.zeros_like(key_sum)
    value_sum[...] = jnp.zeros_like(value_sum)
    for r in range(2):
        trail_recv[r, 1, :, :] = jnp.zeros((COLS, half), BF16)

    def own_step(t, carry):
        @pl.when(t > 0)
        def _():
            pass_on(t, every)

        prepare(t)
        tiles(0)
        for r in range(2):
            early_query[r, t, :, :] = query_part(r, 0, rows)
        return carry

    lax.fori_loop(0, early, own_step, 0)
    for copy in pair_copies:
        copy.wait()
    build_keys(key_other, value_other, rows, partner_seq)

    def other_step(t):
        prepare(t)
        tiles(rows)
        return [early_query[r, t, :, :] + query_part(r, rows, rows) for r in range(2)]

    hand_on(1, other_step(1))
    pass_on(2, every, True)

    def step(t, carry):
        @pl.when(t > early)
        def _():
            pass_on(t, every[1:])

        prepare(t)
        tiles(0)
        tiles(rows)
        pass_on(t + 1, every[:1])
        hand_on(t, [query_part(r, 0, 2 * rows) for r in range(2)])
        return carry

    lax.fori_loop(early, early + 1, step, 0)
    for r, total in enumerate(other_step(0)):
        early_query[r, 0, :, :] = total
    lax.fori_loop(early + 1, nz - 1, step, 0)
    last = nz - 1
    for load in loads[7:]:
        load.wait()
    pass_on(last, every[1:])
    prepare(last)
    part_copies = []
    for c in range(rows // CHUNK):
        here = slice(c * CHUNK, (c + 1) * CHUNK)
        for r in range(2):
            tile(r, rows + c * CHUNK)
        for m, total in enumerate((key_sum, value_sum)):
            part_send[m, here, :] = total[rows + c * CHUNK : rows + (c + 1) * CHUNK, :].astype(BF16)
            copy = remote(
                part_send.at[m, pl.ds(c * CHUNK, CHUNK)],
                part_recv.at[m, pl.ds(c * CHUNK, CHUNK)],
                part_sems.at[0, m, c],
                part_sems.at[1, m, c],
                partner,
            )
            copy.start()
            part_copies.append(copy)
    tiles(0)
    hand_on(last, [query_part(r, 0, 2 * rows) for r in range(2)])
    started = list(part_copies)

    for r in range(2):
        trail_copy(r, nz - 1).wait_recv()
        lanes = slice(r * half, (r + 1) * half)
        low = (early_query[r, 0, :, :] + trail_recv[r, nz, :, :].astype(F32)).astype(BF16)
        flipped_ref[0:COLS, lanes] = low
        grads_ref[lanes, 0:COLS] = jnp.transpose(low.astype(F32)).astype(BF16)

    def launch(copy):
        copy.start()
        started.append(copy)
        return copy

    def at(r, distance):
        return lax.rem(z + distance if r == 0 else z + nz - distance, nz)

    def half_of(r, i):
        return (i + r) % 2

    kinds = (
        (slice(0, COLS), zq_term, zq_send, zq_recv, zq_last),
        (slice(COLS, 3 * COLS), zk_term, zk_send, zk_recv, zk_last),
    )
    z_copies = {}

    def weight_term(kind, z_at, side_at):
        first = pl.multiple_of((z_at * 2 + side_at) * COLS, COLS)
        return dot(flipped_ref[kinds[kind][0], :], input_ref[:, pl.ds(first, COLS)])

    def z_term(kind, i):
        for r in range(2):
            kinds[kind][1][r, i, :, :] = weight_term(kind, at(r, (nz - i) // 2), half_of(r, i))

    def z_message(kind, i, ready=False):
        _, term, send, recv, final = kinds[kind]
        if not ready:
            z_term(kind, i)
        for r in range(2):
            total = term[r, i, :, :]
            if i >= 2:
                z_copies[kind, r, i - 2].wait_recv()
                total = total + recv[r, i - 2, :, :].astype(F32)
            send[r, i, :, :] = total.astype(BF16)
            if i < nz - 3:
                copy = remote(
                    send.at[r, i],
                    recv.at[r, i],
                    z_sems.at[kind, 0, r, i],
                    z_sems.at[kind, 1, r, i],
                    z_ahead[r],
                )
            else:
                copy = remote(
                    send.at[r, i],
                    final.at[r, side],
                    z_sems.at[kind, 0, r, i],
                    last_sems.at[kind, r, side],
                    {"seq": 2 * at(r, 1) + half_of(r, i)},
                )
            z_copies[kind, r, i] = launch(copy)

    near_copies = {}

    def z_near(kind):
        rows_of = kinds[kind][0]
        near_send[rows_of, :] = weight_term(kind, z, 1 - side).astype(BF16)
        near_copies[kind] = launch(
            remote(
                near_send.at[rows_of],
                near_recv.at[rows_of],
                near_sems.at[0, kind],
                near_sems.at[1, kind],
                partner,
            )
        )
        near_term[rows_of, :] = weight_term(kind, z, side)

    def z_final(kind):
        rows_of, _, send, _, final = kinds[kind]
        near_copies[kind].wait_recv()
        total = near_term[rows_of, :] + near_recv[rows_of, :].astype(F32)
        for r in range(2):
            for source in range(2):
                remote(
                    send.at[r, 0],
                    final.at[r, source],
                    z_sems.at[kind, 0, r, 0],
                    last_sems.at[kind, r, source],
                    partner,
                ).wait_recv()
                total = total + final[r, source, :, :].astype(F32)
        for place in range(total.shape[0] // COLS):
            m = rows_of.start // COLS + place
            weight_out[m, :, :] = jnp.transpose(total[place * COLS : (place + 1) * COLS, :])

    def input_term(dx, core_at):
        weights = []
        for y_at in range(2):
            first = pl.multiple_of(((y_at * nx + lax.rem(x + dx, nx)) * 2 + core_at) * COLS, COLS)
            weights.append(
                jnp.concatenate([weight_ref[m, pl.ds(first, COLS), :] for m in range(3)], axis=1)
            )
        return dot_nt(grads_ref[...], jnp.concatenate(weights, axis=0))

    core_copies = {}

    def core_message(dx):
        core_send[dx, :, :] = input_term(dx, 1 - core).astype(BF16)
        core_copies[dx] = launch(
            remote(
                core_send.at[dx],
                core_recv.at[dx],
                core_sems.at[0, dx],
                core_sems.at[1, dx],
                twin,
            )
        )

    x_copies = {}
    fourth = half // 2

    def x_message(kind, r, i):
        send, recv, sems = ((xa_send, xa_recv, xa_sems), (xb_send, xb_recv, xb_sems))[kind]
        x_copies[kind, r, i] = launch(
            remote(send.at[r, i], recv.at[r, i], sems.at[0, r, i], sems.at[1, r, i], x_ahead[r])
        )

    y_copies = {}

    def x_pair(dx):
        total = input_term(dx, core)
        core_copies[dx].wait_recv()
        total = total + core_recv[dx, :, :].astype(F32)
        sides = [total[:, y_at * COLS : (y_at + 1) * COLS] for y_at in range(2)]
        for r in range(2):
            if dx == 2:
                xa_send[r, 0, :, :] = sides[r][:half, :].astype(BF16)
                x_message(0, r, 0)
            elif dx == (1, nx - 1)[r]:
                xa_send[r, 1, :, :] = sides[1 - r][:half, :].astype(BF16)
                x_message(0, r, 1)
                xa_term[r, :, :] = sides[r][:half, :]
            elif dx == 0:
                xa_own[r, :, :] = sides[r][:half, :]
        low, high = sides[0][half:, :], sides[1][half:, :]
        yb_send[dx, :, :] = jnp.where(low_side == 0, high, low).astype(BF16)
        yb_term[dx, :, :] = jnp.where(low_side == 0, low, high)
        y_copies[dx] = launch(
            remote(
                yb_send.at[dx], yb_recv.at[dx], y_sems.at[0, dx], y_sems.at[1, dx], neighbour
            )
        )

    def xa_third(r):
        x_copies[0, r, 0].wait_recv()
        xa_send[r, 2, :, :] = (xa_term[r, :, :] + xa_recv[r, 0, :, :].astype(F32)).astype(BF16)
        x_message(0, r, 2)

    def xb_block(dx):
        y_copies[dx].wait_recv()
        yb_term[dx, :, :] += yb_recv[dx, :, :].astype(F32)

    def xb_part(dx, part):
        return yb_term[dx, part * fourth : (part + 1) * fourth, :]

    def xb_first():
        xb_block(2)
        for r in range(2):
            xb_send[r, 0, :, :] = xb_part(2, r).astype(BF16)
            x_message(1, r, 0)

    def xb_second(r):
        dx = (1, nx - 1)[r]
        xb_block(dx)
        xb_send[r, 1, :, :] = xb_part(dx, 1 - r).astype(BF16)
        x_message(1, r, 1)

    def xb_third(r):
        x_copies[1, r, 0].wait_recv()
        total = xb_part((1, nx - 1)[r], r) + xb_recv[r, 0, :, :].astype(F32)
        xb_send[r, 2, :, :] = total.astype(BF16)
        x_message(1, r, 2)

    def xb_final():
        for part in range(2):
            total = xb_part(0, part)
            for r in range(2):
                i = 2 if r == part else 1
                x_copies[1, r, i].wait_recv()
                total = total + xb_recv[r, i, :, :].astype(F32)
            input_out[half + part * fourth : half + (part + 1) * fourth, :] = total.astype(BF16)

    def xa_final():
        totals = []
        for y_at in range(2):
            total = xa_own[y_at, :, :]
            for r in range(2):
                i = 2 if r == y_at else 1
                x_copies[0, r, i].wait_recv()
                total = total + xa_recv[r, i, :, :].astype(F32)
            totals.append(total)
        ya_send[...] = jnp.where(low_side == 0, totals[1], totals[0]).astype(BF16)
        xa_own[0, :, :] = jnp.where(low_side == 0, totals[0], totals[1])
        return launch(
            remote(ya_send, ya_recv, y_sems.at[0, nx], y_sems.at[1, nx], neighbour)
        )

    def drain(t, carry):
        for r in range(2):
            for part in every:
                slot_copy(r, t, part).wait_send()
            trail_copy(r, t + 1).wait_send()
        return carry

    z_message(0, 0)
    z_message(0, 1)
    z_near(0)
    for i in range(2, nz - 1):
        z_term(0, i)
    lax.fori_loop(0, nz - 1, drain, 0)
    for c in range(rows // CHUNK):
        here = slice(c * CHUNK, (c + 1) * CHUNK)
        for m, total in ((1, key_sum), (2, value_sum)):
            part_copies[2 * c + m - 1].wait_recv()
            low = (total[here, :] + part_recv[m - 1, here, :].astype(F32)).astype(BF16)
            grads_ref[here, m * COLS : (m + 1) * COLS] = low
            flipped_ref[m * COLS : (m + 1) * COLS, here] = jnp.transpose(
                low.astype(F32)
            ).astype(BF16)
    z_message(1, 0)
    z_message(1, 1)
    core_message(2)
    core_message(1)
    x_pair(2)
    z_message(0, 2, True)
    z_message(0, 3, True)
    core_message(3)
    x_pair(1)
    z_term(1, 2)
    z_term(1, 3)
    core_message(0)
    z_message(1, 2, True)
    z_message(1, 3, True)
    x_pair(3)
    x_pair(0)
    z_message(0, 4, True)
    z_message(0, 5, True)
    xb_first()
    xa_third(0)
    xa_third(1)
    z_term(1, 4)
    z_term(1, 5)
    z_message(1, 4, True)
    z_message(1, 5, True)
    z_near(1)
    z_term(1, 6)
    xb_second(0)
    xb_second(1)
    z_message(0, 6, True)
    z_message(1, 6, True)
    xb_third(0)
    xb_third(1)
    xb_block(0)
    y_copy = xa_final()
    xb_final()
    z_final(0)
    y_copy.wait_recv()
    input_out[0:half, :] = (xa_own[0, :, :] + ya_recv[...].astype(F32)).astype(BF16)
    z_final(1)
    for copy in started:
        copy.wait_send()


def local(
    nz,
    nx,
    layer_input,
    qkv_weight,
    queries,
    key_states,
    value_states,
    attn_out,
    grad_out,
    log_sum_exp,
    frames,
):
    rows = queries.shape[0]
    half = rows // 2
    wide = 3 * COLS
    vmem = pl.BlockSpec(memory_space=pltpu.VMEM)
    anywhere = pl.BlockSpec(memory_space=pltpu.HBM)
    dma = pltpu.SemaphoreType.DMA
    stat = log_sum_exp.T

    def low(*shape):
        return pltpu.VMEM(shape, BF16)

    def full(*shape):
        return pltpu.VMEM(shape, F32)

    return pl.pallas_call(
        functools.partial(backward_kernel, nz, nx),
        out_shape=(
            pltpu.VMEM((rows, COLS), BF16),
            pltpu.VMEM((3, COLS, COLS), F32),
        ),
        in_specs=[anywhere] * 9,
        out_specs=(vmem, vmem),
        scratch_shapes=[
            pltpu.SMEM(frames.shape, jnp.int32),
            full(*stat.shape),
            low(rows, COLS),
            low(rows, COLS),
            low(rows, COLS),
            low(rows, COLS),
            low(rows, COLS),
            low(*layer_input.shape),
            low(*qkv_weight.shape),
            low(rows, COLS),
            low(rows, COLS),
            low(2, nz, 2 * COLS + 16, half),
            low(2, nz, COLS, half),
            low(2, nz + 1, COLS, half),
            low(2, 2 * rows, COLS),
            low(2, 2 * rows, COLS),
            low(COLS, 2 * rows),
            low(2, 4, COLS, half),
            low(2, 2, COLS, 2 * half),
            low(2, 2, 2 * rows, half),
            full(2 * rows, COLS),
            full(2 * rows, COLS),
            full(2, 2, COLS, half),
            low(2, rows, COLS),
            low(2, rows, COLS),
            low(rows, wide),
            low(wide, rows),
            low(nx, rows, 2 * COLS),
            low(nx, rows, 2 * COLS),
            low(2, 3, half, COLS),
            low(2, 3, half, COLS),
            full(2, half, COLS),
            full(2, half, COLS),
            low(2, 3, half // 2, COLS),
            low(2, 3, half // 2, COLS),
            low(nx, half, COLS),
            low(nx, half, COLS),
            full(nx, half, COLS),
            low(half, COLS),
            low(half, COLS),
            full(2, nz - 1, COLS, COLS),
            low(2, nz - 1, COLS, COLS),
            low(2, nz - 3, COLS, COLS),
            low(2, 2, COLS, COLS),
            full(2, nz - 1, 2 * COLS, COLS),
            low(2, nz - 1, 2 * COLS, COLS),
            low(2, nz - 3, 2 * COLS, COLS),
            low(2, 2, 2 * COLS, COLS),
            full(wide, COLS),
            low(wide, COLS),
            low(wide, COLS),
            dma((9,)),
            dma((2, len(PIECES) - 1, 2, nz)),
            dma((2, 2, nz + 1)),
            dma((2, 2)),
            dma((2, 2, rows // CHUNK)),
            dma((2, nx)),
            dma((2, 2, 3)),
            dma((2, 2, 3)),
            dma((2, nx + 1)),
            dma((2, 2, 2, nz - 1)),
            dma((2, 2, 2)),
            dma((2, 2)),
        ],
        compiler_params=pltpu.CompilerParams(
            collective_id=0, has_side_effects=True, vmem_limit_bytes=48 * 2**20
        ),
        name="attention_backward",
    )(
        *(
            pltpu.with_memory_space_constraint(array, pltpu.HBM)
            for array in (
                frames,
                stat,
                queries,
                key_states,
                value_states,
                attn_out,
                grad_out,
                layer_input,
                qkv_weight,
            )
        )
    )


def solution(mesh):
    nz = mesh.shape["seq"] // 2
    nx = mesh.shape["head"] // 4
    placed = (
        P("seq", None),
        P(None, None, "head"),
        P("seq", "head"),
        P("seq", "head"),
        P("seq", "head"),
        P("seq", "head"),
        P("seq", "head"),
        P("seq", "head"),
        P(),
    )
    return jax.shard_map(
        functools.partial(local, nz, nx),
        mesh=mesh,
        in_specs=placed,
        out_specs=(P("seq", "head"), P(None, "seq", "head")),
        check_vma=False,
    )
```

```python
import functools

import jax
import jax.numpy as jnp
from jax import lax
from jax.experimental import pallas as pl
from jax.experimental.pallas import tpu as pltpu
from jax.sharding import PartitionSpec as P

BLOCK = 64
HEAD_SIZE = 64
COLS = 2 * HEAD_SIZE
FRAMES = 32
CHUNK = 256
HIDDEN = -16384.0
LOG2E = 1.4426950408889634
MESH = pl.DeviceIdType.MESH
PIECES = (0, 128, 272)
BF16 = jnp.bfloat16
F32 = jnp.float32


def dot(left, right):
    return jnp.dot(left, right, preferred_element_type=F32)


def dot_nt(left, right):
    return lax.dot_general(left, right, (((1,), (1,)), ((), ())), preferred_element_type=F32)


def greet(peers):
    barrier = pltpu.get_barrier_semaphore()
    for peer in peers:
        pl.semaphore_signal(barrier, inc=1, device_id=peer, device_id_type=MESH)


def remote(source, target, send_sem, recv_sem, peer):
    return pltpu.make_async_remote_copy(
        src_ref=source,
        dst_ref=target,
        send_sem=send_sem,
        recv_sem=recv_sem,
        device_id=peer,
        device_id_type=MESH,
    )


def backward_kernel(
    nz,
    nx,
    frames_hbm,
    stat_hbm,
    query_hbm,
    key_hbm,
    value_hbm,
    out_hbm,
    grad_hbm,
    input_hbm,
    weight_hbm,
    input_out,
    weight_out,
    frames_ref,
    stat_ref,
    query_ref,
    key_ref,
    value_ref,
    out_ref,
    grad_ref,
    input_ref,
    weight_ref,
    key_other,
    value_other,
    slots,
    trail_send,
    trail_recv,
    key_wide,
    value_wide,
    key_flip,
    fixed,
    paired,
    score_low,
    key_sum,
    value_sum,
    early_query,
    part_send,
    part_recv,
    grads_ref,
    flipped_ref,
    core_send,
    core_recv,
    xa_send,
    xa_recv,
    xa_term,
    xa_own,
    xb_send,
    xb_recv,
    yb_send,
    yb_recv,
    yb_term,
    ya_send,
    ya_recv,
    zq_term,
    zq_send,
    zq_recv,
    zq_last,
    zk_term,
    zk_send,
    zk_recv,
    zk_last,
    near_term,
    near_send,
    near_recv,
    load_sems,
    slot_sems,
    trail_sems,
    pair_sems,
    part_sems,
    core_sems,
    xa_sems,
    xb_sems,
    y_sems,
    z_sems,
    last_sems,
    near_sems,
):
    loads = [
        pltpu.make_async_copy(source, target, load_sems.at[i])
        for i, (source, target) in enumerate(
            (
                (query_hbm, query_ref),
                (grad_hbm, grad_ref),
                (out_hbm, out_ref),
                (stat_hbm, stat_ref),
                (key_hbm, key_ref),
                (value_hbm, value_ref),
                (frames_hbm, frames_ref),
                (input_hbm, input_ref),
                (weight_hbm, weight_ref),
            )
        )
    ]
    for load in loads:
        load.start()

    rows = query_ref.shape[0]
    half = rows // 2
    blocks = rows // BLOCK
    count = 2 * nz
    seq = lax.axis_index("seq")
    head = lax.axis_index("head")
    side = lax.rem(seq, 2)
    z = seq // 2
    partner_seq = seq + 1 - 2 * side
    partner = {"seq": partner_seq}
    z_ahead = ({"seq": lax.rem(seq + 2, count)}, {"seq": lax.rem(seq + count - 2, count)})
    core = lax.rem(head, 2)
    x = lax.rem(head // 2, nx)
    low_side = head // (2 * nx)
    twin = {"head": head + 1 - 2 * core}
    plane = low_side * 2 * nx + core
    x_ahead = (
        {"head": plane + 2 * lax.rem(x + 1, nx)},
        {"head": plane + 2 * lax.rem(x + nx - 1, nx)},
    )
    neighbour = {"head": (1 - low_side) * 2 * nx + 2 * x + core}
    slants = [{"seq": 2 * lax.rem(z + dz, nz) + 1 - side} for dz in (1, nz - 1)]
    peers = (*z_ahead, partner, *slants, twin, neighbour, *x_ahead)
    greet(peers)

    pair_copies = [
        remote(key_hbm, key_other, pair_sems.at[0, 0], pair_sems.at[1, 0], partner),
        remote(value_hbm, value_other, pair_sems.at[0, 1], pair_sems.at[1, 1], partner),
    ]
    def slot_copy(r, t, part):
        here = pl.ds(PIECES[part], PIECES[part + 1] - PIECES[part])
        return remote(
            slots.at[r, t, here],
            slots.at[r, t + 1, here],
            slot_sems.at[0, part, r, t],
            slot_sems.at[1, part, r, t + 1],
            z_ahead[r],
        )

    def trail_copy(r, t):
        return remote(
            trail_send.at[r, t],
            trail_recv.at[r, t + 1],
            trail_sems.at[0, r, t],
            trail_sems.at[1, r, t + 1],
            z_ahead[r],
        )

    every = range(len(PIECES) - 1)

    def forward(t, part):
        for r in range(2):
            slot_copy(r, t, part).start()

    loads[0].wait()
    query_flip = jnp.transpose(query_ref[...].astype(F32) * (HEAD_SIZE**-0.5))
    for r in range(2):
        slots[r, 0, 0:COLS, :] = query_flip[:, r * half : (r + 1) * half].astype(BF16)
    pl.semaphore_wait(pltpu.get_barrier_semaphore(), len(peers))
    for copy in pair_copies:
        copy.start()
    forward(0, 0)
    for load in loads[1:4]:
        load.wait()
    grad_wide = grad_ref[...].astype(F32)
    grad_flip = jnp.transpose(grad_wide)
    delta_flip = jnp.transpose(grad_wide * out_ref[...].astype(F32))
    aux_row = lax.broadcasted_iota(jnp.int32, (16, rows), 0)
    aux = jnp.zeros((16, rows), F32)
    for h in range(2):
        delta = jnp.sum(
            delta_flip[h * HEAD_SIZE : (h + 1) * HEAD_SIZE, :], axis=0, keepdims=True
        )
        for first, value in ((3 * h, stat_ref[h : h + 1, :]), (6 + 3 * h, delta)):
            rest = value
            for place in range(3):
                piece = rest.astype(BF16).astype(F32)
                aux = jnp.where(aux_row == first + place, piece, aux)
                rest = rest - piece
    for r in range(2):
        lanes = slice(r * half, (r + 1) * half)
        slots[r, 0, COLS : 2 * COLS, :] = grad_flip[:, lanes].astype(BF16)
        slots[r, 0, 2 * COLS : 2 * COLS + 16, :] = aux[:, lanes].astype(BF16)

    lane = lax.broadcasted_iota(jnp.int32, (BLOCK, COLS), 1)
    inner = lax.rem(lane, HEAD_SIZE)

    def build_keys(keys_from, values_from, base, owner):
        for b in range(blocks):
            here = slice(b * BLOCK, (b + 1) * BLOCK)
            there = slice(base + b * BLOCK, base + (b + 1) * BLOCK)
            frame = frames_ref[owner * blocks + b]
            keys = keys_from[here, :].astype(F32)
            values = values_from[here, :].astype(F32)
            for h in range(2):
                mine = (lane >= h * HEAD_SIZE) & (lane < (h + 1) * HEAD_SIZE)
                stat_at = (inner >= FRAMES + 3 * h) & (inner < FRAMES + 3 * h + 3)
                delta_at = (inner >= FRAMES + 6 + 3 * h) & (inner < FRAMES + 9 + 3 * h)
                key_more = jnp.where(inner == frame, 1.0, jnp.where(stat_at, -1.0, 0.0))
                value_more = jnp.where(delta_at, -1.0, 0.0)
                key_wide[h, there, :] = jnp.where(mine, keys, key_more).astype(BF16)
                value_wide[h, there, :] = jnp.where(mine, values, value_more).astype(BF16)
        key_flip[:, base : base + rows] = jnp.transpose(
            keys_from[...].astype(F32) * (HEAD_SIZE**-0.5)
        ).astype(BF16)

    frame_row = lax.broadcasted_iota(jnp.int32, (FRAMES, half), 0)
    frame_lane = lax.broadcasted_iota(jnp.int32, (FRAMES, half), 1)

    def prepare(t):
        for r, owner in enumerate((lax.rem(seq + 2 * (nz - t), count), lax.rem(seq + 2 * t, count))):
            first = owner * blocks + r * (blocks // 2)
            seen = jnp.full((FRAMES, half), frames_ref[first + blocks // 2 - 1], jnp.int32)
            for i in range(blocks // 2 - 2, -1, -1):
                seen = jnp.where(frame_lane < (i + 1) * BLOCK, frames_ref[first + i], seen)
            hidden = jnp.where(frame_row > seen, HIDDEN, 0.0).astype(BF16)
            extra = jnp.concatenate(
                [hidden, slots[r, t, 2 * COLS : 2 * COLS + 16, :], jnp.zeros((16, half), BF16)],
                axis=0,
            )
            zero = jnp.zeros((HEAD_SIZE, half), BF16)
            for which in range(2):
                low = slots[r, t, which * COLS : which * COLS + HEAD_SIZE, :]
                high = slots[r, t, which * COLS + HEAD_SIZE : (which + 1) * COLS, :]
                fixed[r, 2 * which, :, :] = jnp.concatenate([low, extra], axis=0)
                fixed[r, 2 * which + 1, :, :] = jnp.concatenate([extra, high], axis=0)
                paired[r, which, :, :] = jnp.concatenate(
                    [
                        jnp.concatenate([low, zero], axis=1),
                        jnp.concatenate([zero, high], axis=1),
                    ],
                    axis=0,
                )

    def tile(r, start):
        here = pl.ds(start, CHUNK)
        probs, scores = [], []
        for h in range(2):
            score = dot(key_wide[h, here, :], fixed[r, h, :, :])
            prob = jnp.exp2(score * LOG2E)
            prob_grad = dot(value_wide[h, here, :], fixed[r, 2 + h, :, :])
            score_grad = (prob * prob_grad).astype(BF16)
            score_low[r, h, here, :] = score_grad
            probs.append(prob.astype(BF16))
            scores.append(score_grad)
        value_sum[here, :] += dot_nt(jnp.concatenate(probs, axis=1), paired[r, 1, :, :])
        key_sum[here, :] += dot_nt(jnp.concatenate(scores, axis=1), paired[r, 0, :, :])

    def tiles(first):
        for c in range(rows // CHUNK):
            for r in range(2):
                tile(r, first + c * CHUNK)

    def query_part(r, first, length):
        return jnp.concatenate(
            [
                dot(
                    key_flip[h * HEAD_SIZE : (h + 1) * HEAD_SIZE, first : first + length],
                    score_low[r, h, first : first + length, :],
                )
                for h in range(2)
            ],
            axis=0,
        )

    def pass_on(t, parts, onward=None):
        for part in parts:
            for r in range(2):
                slot_copy(r, t - 1, part).wait_recv()
                if onward is None:

                    @pl.when(t < nz - 1)
                    def _(r=r, part=part):
                        slot_copy(r, t, part).start()

                elif onward:
                    slot_copy(r, t, part).start()

    def hand_on(t, totals):
        if not isinstance(t, int) or t > 1:
            for r in range(2):
                trail_copy(r, t - 1).wait_recv()

        for r in range(2):
            total = totals[r] + trail_recv[r, t, :, :].astype(F32)
            trail_send[r, t, :, :] = total.astype(BF16)
            trail_copy(r, t).start()

    early = min(2, nz - 1)
    forward(0, 1)
    for load in loads[4:7]:
        load.wait()
    build_keys(key_ref, value_ref, 0, seq)
    key_sum[...] = jnp.zeros_like(key_sum)
    value_sum[...] = jnp.zeros_like(value_sum)
    for r in range(2):
        trail_recv[r, 1, :, :] = jnp.zeros((COLS, half), BF16)

    def own_step(t, carry):
        @pl.when(t > 0)
        def _():
            pass_on(t, every)

        prepare(t)
        tiles(0)
        for r in range(2):
            early_query[r, t, :, :] = query_part(r, 0, rows)
        return carry

    lax.fori_loop(0, early, own_step, 0)
    for copy in pair_copies:
        copy.wait()
    build_keys(key_other, value_other, rows, partner_seq)

    def other_step(t):
        prepare(t)
        tiles(rows)
        return [early_query[r, t, :, :] + query_part(r, rows, rows) for r in range(2)]

    hand_on(1, other_step(1))
    pass_on(2, every, True)

    def step(t, carry):
        @pl.when(t > early)
        def _():
            pass_on(t, every[1:])

        prepare(t)
        tiles(0)
        tiles(rows)
        pass_on(t + 1, every[:1])
        hand_on(t, [query_part(r, 0, 2 * rows) for r in range(2)])
        return carry

    lax.fori_loop(early, early + 1, step, 0)
    for r, total in enumerate(other_step(0)):
        early_query[r, 0, :, :] = total
    lax.fori_loop(early + 1, nz - 1, step, 0)
    last = nz - 1
    for load in loads[7:]:
        load.wait()
    pass_on(last, every[1:], False)
    prepare(last)
    part_copies = []
    for c in range(rows // CHUNK):
        here = slice(c * CHUNK, (c + 1) * CHUNK)
        for r in range(2):
            tile(r, rows + c * CHUNK)
        for m, total in enumerate((key_sum, value_sum)):
            part_send[m, here, :] = total[rows + c * CHUNK : rows + (c + 1) * CHUNK, :].astype(BF16)
            copy = remote(
                part_send.at[m, pl.ds(c * CHUNK, CHUNK)],
                part_recv.at[m, pl.ds(c * CHUNK, CHUNK)],
                part_sems.at[0, m, c],
                part_sems.at[1, m, c],
                partner,
            )
            copy.start()
            part_copies.append(copy)
    tiles(0)
    hand_on(last, [query_part(r, 0, 2 * rows) for r in range(2)])
    started = list(part_copies)

    for r in range(2):
        trail_copy(r, nz - 1).wait_recv()
        lanes = slice(r * half, (r + 1) * half)
        low = (early_query[r, 0, :, :] + trail_recv[r, nz, :, :].astype(F32)).astype(BF16)
        flipped_ref[0:COLS, lanes] = low
        grads_ref[lanes, 0:COLS] = jnp.transpose(low.astype(F32)).astype(BF16)

    def launch(copy):
        copy.start()
        started.append(copy)
        return copy

    def at(r, distance):
        return lax.rem(z + distance if r == 0 else z + nz - distance, nz)

    def half_of(r, i):
        return (i + r) % 2

    kinds = (
        (slice(0, COLS), zq_term, zq_send, zq_recv, zq_last),
        (slice(COLS, 3 * COLS), zk_term, zk_send, zk_recv, zk_last),
    )
    z_copies = {}

    def weight_term(kind, z_at, side_at):
        first = pl.multiple_of((z_at * 2 + side_at) * COLS, COLS)
        return dot(flipped_ref[kinds[kind][0], :], input_ref[:, pl.ds(first, COLS)])

    def z_term(kind, i):
        for r in range(2):
            kinds[kind][1][r, i, :, :] = weight_term(kind, at(r, (nz - i) // 2), half_of(r, i))

    def z_message(kind, i, ready=False):
        _, term, send, recv, final = kinds[kind]
        if not ready:
            z_term(kind, i)
        for r in range(2):
            total = term[r, i, :, :]
            if i >= 2:
                z_copies[kind, r, i - 2].wait_recv()
                total = total + recv[r, i - 2, :, :].astype(F32)
            send[r, i, :, :] = total.astype(BF16)
            if i < nz - 3:
                copy = remote(
                    send.at[r, i],
                    recv.at[r, i],
                    z_sems.at[kind, 0, r, i],
                    z_sems.at[kind, 1, r, i],
                    z_ahead[r],
                )
            else:
                copy = remote(
                    send.at[r, i],
                    final.at[r, side],
                    z_sems.at[kind, 0, r, i],
                    last_sems.at[kind, r, side],
                    {"seq": 2 * at(r, 1) + half_of(r, i)},
                )
            z_copies[kind, r, i] = launch(copy)

    near_copies = {}

    def z_near(kind):
        rows_of = kinds[kind][0]
        near_send[rows_of, :] = weight_term(kind, z, 1 - side).astype(BF16)
        near_copies[kind] = launch(
            remote(
                near_send.at[rows_of],
                near_recv.at[rows_of],
                near_sems.at[0, kind],
                near_sems.at[1, kind],
                partner,
            )
        )
        near_term[rows_of, :] = weight_term(kind, z, side)

    def z_final(kind):
        rows_of, _, send, _, final = kinds[kind]
        near_copies[kind].wait_recv()
        total = near_term[rows_of, :] + near_recv[rows_of, :].astype(F32)
        for r in range(2):
            for source in range(2):
                remote(
                    send.at[r, 0],
                    final.at[r, source],
                    z_sems.at[kind, 0, r, 0],
                    last_sems.at[kind, r, source],
                    partner,
                ).wait_recv()
                total = total + final[r, source, :, :].astype(F32)
        for place in range(total.shape[0] // COLS):
            m = rows_of.start // COLS + place
            weight_out[m, :, :] = jnp.transpose(total[place * COLS : (place + 1) * COLS, :])

    def input_term(dx, core_at):
        weights = []
        for y_at in range(2):
            first = pl.multiple_of(((y_at * nx + lax.rem(x + dx, nx)) * 2 + core_at) * COLS, COLS)
            weights.append(
                jnp.concatenate([weight_ref[m, pl.ds(first, COLS), :] for m in range(3)], axis=1)
            )
        return dot_nt(grads_ref[...], jnp.concatenate(weights, axis=0))

    core_copies = {}

    def core_message(dx):
        core_send[dx, :, :] = input_term(dx, 1 - core).astype(BF16)
        core_copies[dx] = launch(
            remote(
                core_send.at[dx],
                core_recv.at[dx],
                core_sems.at[0, dx],
                core_sems.at[1, dx],
                twin,
            )
        )

    x_copies = {}
    fourth = half // 2

    def x_message(kind, r, i):
        send, recv, sems = ((xa_send, xa_recv, xa_sems), (xb_send, xb_recv, xb_sems))[kind]
        x_copies[kind, r, i] = launch(
            remote(send.at[r, i], recv.at[r, i], sems.at[0, r, i], sems.at[1, r, i], x_ahead[r])
        )

    y_copies = {}

    def x_pair(dx):
        total = input_term(dx, core)
        core_copies[dx].wait_recv()
        total = total + core_recv[dx, :, :].astype(F32)
        sides = [total[:, y_at * COLS : (y_at + 1) * COLS] for y_at in range(2)]
        for r in range(2):
            if dx == 2:
                xa_send[r, 0, :, :] = sides[r][:half, :].astype(BF16)
                x_message(0, r, 0)
            elif dx == (1, nx - 1)[r]:
                xa_send[r, 1, :, :] = sides[1 - r][:half, :].astype(BF16)
                x_message(0, r, 1)
                xa_term[r, :, :] = sides[r][:half, :]
            elif dx == 0:
                xa_own[r, :, :] = sides[r][:half, :]
        low, high = sides[0][half:, :], sides[1][half:, :]
        yb_send[dx, :, :] = jnp.where(low_side == 0, high, low).astype(BF16)
        yb_term[dx, :, :] = jnp.where(low_side == 0, low, high)
        y_copies[dx] = launch(
            remote(
                yb_send.at[dx], yb_recv.at[dx], y_sems.at[0, dx], y_sems.at[1, dx], neighbour
            )
        )

    def xa_third(r):
        x_copies[0, r, 0].wait_recv()
        xa_send[r, 2, :, :] = (xa_term[r, :, :] + xa_recv[r, 0, :, :].astype(F32)).astype(BF16)
        x_message(0, r, 2)

    def xb_block(dx):
        y_copies[dx].wait_recv()
        yb_term[dx, :, :] += yb_recv[dx, :, :].astype(F32)

    def xb_part(dx, part):
        return yb_term[dx, part * fourth : (part + 1) * fourth, :]

    def xb_first():
        xb_block(2)
        for r in range(2):
            xb_send[r, 0, :, :] = xb_part(2, r).astype(BF16)
            x_message(1, r, 0)

    def xb_second(r):
        dx = (1, nx - 1)[r]
        xb_block(dx)
        xb_send[r, 1, :, :] = xb_part(dx, 1 - r).astype(BF16)
        x_message(1, r, 1)

    def xb_third(r):
        x_copies[1, r, 0].wait_recv()
        total = xb_part((1, nx - 1)[r], r) + xb_recv[r, 0, :, :].astype(F32)
        xb_send[r, 2, :, :] = total.astype(BF16)
        x_message(1, r, 2)

    def xb_final():
        for part in range(2):
            total = xb_part(0, part)
            for r in range(2):
                i = 2 if r == part else 1
                x_copies[1, r, i].wait_recv()
                total = total + xb_recv[r, i, :, :].astype(F32)
            input_out[half + part * fourth : half + (part + 1) * fourth, :] = total.astype(BF16)

    def xa_final():
        totals = []
        for y_at in range(2):
            total = xa_own[y_at, :, :]
            for r in range(2):
                i = 2 if r == y_at else 1
                x_copies[0, r, i].wait_recv()
                total = total + xa_recv[r, i, :, :].astype(F32)
            totals.append(total)
        ya_send[...] = jnp.where(low_side == 0, totals[1], totals[0]).astype(BF16)
        xa_own[0, :, :] = jnp.where(low_side == 0, totals[0], totals[1])
        return launch(
            remote(ya_send, ya_recv, y_sems.at[0, nx], y_sems.at[1, nx], neighbour)
        )

    def drain(t, carry):
        for r in range(2):
            for part in every:
                slot_copy(r, t, part).wait_send()
            trail_copy(r, t + 1).wait_send()
        return carry

    z_message(0, 0)
    z_message(0, 1)
    z_near(0)
    for i in range(2, nz - 1):
        z_term(0, i)
    lax.fori_loop(0, nz - 1, drain, 0)
    for c in range(rows // CHUNK):
        here = slice(c * CHUNK, (c + 1) * CHUNK)
        for m, total in ((1, key_sum), (2, value_sum)):
            part_copies[2 * c + m - 1].wait_recv()
            low = (total[here, :] + part_recv[m - 1, here, :].astype(F32)).astype(BF16)
            grads_ref[here, m * COLS : (m + 1) * COLS] = low
            flipped_ref[m * COLS : (m + 1) * COLS, here] = jnp.transpose(
                low.astype(F32)
            ).astype(BF16)
    core_message(2)
    core_message(3)
    z_message(1, 0)
    core_message(1)
    z_message(1, 1)
    x_pair(2)
    core_message(0)
    z_term(1, 2)
    z_message(0, 2, True)
    x_pair(3)
    z_near(1)
    z_message(1, 2, True)
    x_pair(1)
    z_term(1, 4)
    z_message(0, 3, True)
    z_term(1, 6)
    z_term(1, 3)
    xa_third(0)
    xa_third(1)
    z_term(1, 5)
    xb_first()
    z_message(1, 3, True)
    xb_second(1)
    x_pair(0)
    z_message(0, 4, True)
    z_message(0, 5, True)
    z_message(1, 4, True)
    y_copy = xa_final()
    xb_second(0)
    z_message(1, 5, True)
    z_message(0, 6, True)
    xb_block(0)
    xb_third(0)
    xb_third(1)
    z_message(1, 6, True)
    y_copy.wait_recv()
    input_out[0:half, :] = (xa_own[0, :, :] + ya_recv[...].astype(F32)).astype(BF16)
    z_final(0)
    xb_final()
    z_final(1)
    for copy in started:
        copy.wait_send()


def local(
    nz,
    nx,
    layer_input,
    qkv_weight,
    queries,
    key_states,
    value_states,
    attn_out,
    grad_out,
    log_sum_exp,
    frames,
):
    rows = queries.shape[0]
    half = rows // 2
    wide = 3 * COLS
    vmem = pl.BlockSpec(memory_space=pltpu.VMEM)
    anywhere = pl.BlockSpec(memory_space=pltpu.HBM)
    dma = pltpu.SemaphoreType.DMA
    stat = log_sum_exp.T

    def low(*shape):
        return pltpu.VMEM(shape, BF16)

    def full(*shape):
        return pltpu.VMEM(shape, F32)

    return pl.pallas_call(
        functools.partial(backward_kernel, nz, nx),
        out_shape=(
            pltpu.VMEM((rows, COLS), BF16),
            pltpu.VMEM((3, COLS, COLS), F32),
        ),
        in_specs=[anywhere] * 9,
        out_specs=(vmem, vmem),
        scratch_shapes=[
            pltpu.SMEM(frames.shape, jnp.int32),
            full(*stat.shape),
            low(rows, COLS),
            low(rows, COLS),
            low(rows, COLS),
            low(rows, COLS),
            low(rows, COLS),
            low(*layer_input.shape),
            low(*qkv_weight.shape),
            low(rows, COLS),
            low(rows, COLS),
            low(2, nz, 2 * COLS + 16, half),
            low(2, nz, COLS, half),
            low(2, nz + 1, COLS, half),
            low(2, 2 * rows, COLS),
            low(2, 2 * rows, COLS),
            low(COLS, 2 * rows),
            low(2, 4, COLS, half),
            low(2, 2, COLS, 2 * half),
            low(2, 2, 2 * rows, half),
            full(2 * rows, COLS),
            full(2 * rows, COLS),
            full(2, 2, COLS, half),
            low(2, rows, COLS),
            low(2, rows, COLS),
            low(rows, wide),
            low(wide, rows),
            low(nx, rows, 2 * COLS),
            low(nx, rows, 2 * COLS),
            low(2, 3, half, COLS),
            low(2, 3, half, COLS),
            full(2, half, COLS),
            full(2, half, COLS),
            low(2, 3, half // 2, COLS),
            low(2, 3, half // 2, COLS),
            low(nx, half, COLS),
            low(nx, half, COLS),
            full(nx, half, COLS),
            low(half, COLS),
            low(half, COLS),
            full(2, nz - 1, COLS, COLS),
            low(2, nz - 1, COLS, COLS),
            low(2, nz - 3, COLS, COLS),
            low(2, 2, COLS, COLS),
            full(2, nz - 1, 2 * COLS, COLS),
            low(2, nz - 1, 2 * COLS, COLS),
            low(2, nz - 3, 2 * COLS, COLS),
            low(2, 2, 2 * COLS, COLS),
            full(wide, COLS),
            low(wide, COLS),
            low(wide, COLS),
            dma((9,)),
            dma((2, len(PIECES) - 1, 2, nz)),
            dma((2, 2, nz + 1)),
            dma((2, 2)),
            dma((2, 2, rows // CHUNK)),
            dma((2, nx)),
            dma((2, 2, 3)),
            dma((2, 2, 3)),
            dma((2, nx + 1)),
            dma((2, 2, 2, nz - 1)),
            dma((2, 2, 2)),
            dma((2, 2)),
        ],
        compiler_params=pltpu.CompilerParams(
            collective_id=0, has_side_effects=True, vmem_limit_bytes=48 * 2**20
        ),
        name="attention_backward",
    )(
        *(
            pltpu.with_memory_space_constraint(array, pltpu.HBM)
            for array in (
                frames,
                stat,
                queries,
                key_states,
                value_states,
                attn_out,
                grad_out,
                layer_input,
                qkv_weight,
            )
        )
    )


def solution(mesh):
    nz = mesh.shape["seq"] // 2
    nx = mesh.shape["head"] // 4
    placed = (
        P("seq", None),
        P(None, None, "head"),
        P("seq", "head"),
        P("seq", "head"),
        P("seq", "head"),
        P("seq", "head"),
        P("seq", "head"),
        P("seq", "head"),
        P(),
    )
    return jax.shard_map(
        functools.partial(local, nz, nx),
        mesh=mesh,
        in_specs=placed,
        out_specs=(P("seq", "head"), P(None, "seq", "head")),
        check_vma=False,
    )
```

```python
import functools

import jax
import jax.numpy as jnp
from jax import lax
from jax.experimental import pallas as pl
from jax.experimental.pallas import tpu as pltpu
from jax.sharding import PartitionSpec as P

BLOCK = 64
HEAD_SIZE = 64
COLS = 2 * HEAD_SIZE
FRAMES = 32
CHUNK = 256
HIDDEN = -16384.0
LOG2E = 1.4426950408889634
MESH = pl.DeviceIdType.MESH
PIECES = (0, 128, 272)
BF16 = jnp.bfloat16
F32 = jnp.float32


def dot(left, right):
    return jnp.dot(left, right, preferred_element_type=F32)


def dot_nt(left, right):
    return lax.dot_general(left, right, (((1,), (1,)), ((), ())), preferred_element_type=F32)


def greet(peers):
    barrier = pltpu.get_barrier_semaphore()
    for peer in peers:
        pl.semaphore_signal(barrier, inc=1, device_id=peer, device_id_type=MESH)


def remote(source, target, send_sem, recv_sem, peer):
    return pltpu.make_async_remote_copy(
        src_ref=source,
        dst_ref=target,
        send_sem=send_sem,
        recv_sem=recv_sem,
        device_id=peer,
        device_id_type=MESH,
    )


def backward_kernel(
    nz,
    nx,
    frames_hbm,
    stat_hbm,
    query_hbm,
    key_hbm,
    value_hbm,
    out_hbm,
    grad_hbm,
    input_hbm,
    weight_hbm,
    input_out,
    weight_out,
    frames_ref,
    stat_ref,
    query_ref,
    key_ref,
    value_ref,
    out_ref,
    grad_ref,
    input_ref,
    weight_ref,
    key_other,
    value_other,
    slots,
    trail_send,
    trail_recv,
    key_wide,
    value_wide,
    key_flip,
    fixed,
    paired,
    score_low,
    key_sum,
    value_sum,
    early_query,
    part_send,
    part_recv,
    grads_ref,
    flipped_ref,
    core_send,
    core_recv,
    xa_send,
    xa_recv,
    xa_term,
    xa_own,
    xb_send,
    xb_recv,
    yb_send,
    yb_recv,
    yb_term,
    ya_send,
    ya_recv,
    zq_term,
    zq_send,
    zq_recv,
    zq_last,
    zk_term,
    zk_send,
    zk_recv,
    zk_last,
    near_term,
    near_send,
    near_recv,
    load_sems,
    slot_sems,
    trail_sems,
    pair_sems,
    part_sems,
    core_sems,
    xa_sems,
    xb_sems,
    y_sems,
    z_sems,
    last_sems,
    near_sems,
):
    rows = query_ref.shape[0]
    half = rows // 2
    blocks = rows // BLOCK
    count = 2 * nz
    seq = lax.axis_index("seq")
    head = lax.axis_index("head")
    side = lax.rem(seq, 2)
    z = seq // 2
    partner_seq = seq + 1 - 2 * side
    partner = {"seq": partner_seq}
    z_ahead = ({"seq": lax.rem(seq + 2, count)}, {"seq": lax.rem(seq + count - 2, count)})
    core = lax.rem(head, 2)
    x = lax.rem(head // 2, nx)
    low_side = head // (2 * nx)
    twin = {"head": head + 1 - 2 * core}
    plane = low_side * 2 * nx + core
    x_ahead = (
        {"head": plane + 2 * lax.rem(x + 1, nx)},
        {"head": plane + 2 * lax.rem(x + nx - 1, nx)},
    )
    neighbour = {"head": (1 - low_side) * 2 * nx + 2 * x + core}
    slants = [{"seq": 2 * lax.rem(z + dz, nz) + 1 - side} for dz in (1, nz - 1)]
    peers = (*z_ahead, partner, *slants, twin, neighbour, *x_ahead)
    greet(peers)
    loads = [
        pltpu.make_async_copy(source, target, load_sems.at[i])
        for i, (source, target) in enumerate(
            (
                (query_hbm, query_ref),
                (grad_hbm, grad_ref),
                (out_hbm, out_ref),
                (stat_hbm, stat_ref),
                (key_hbm, key_ref),
                (value_hbm, value_ref),
                (frames_hbm, frames_ref),
                (input_hbm, input_ref),
                (weight_hbm, weight_ref),
            )
        )
    ]
    for load in loads[:7]:
        load.start()


    pair_copies = [
        remote(key_hbm, key_other, pair_sems.at[0, 0], pair_sems.at[1, 0], partner),
        remote(value_hbm, value_other, pair_sems.at[0, 1], pair_sems.at[1, 1], partner),
    ]
    def slot_copy(r, t, part):
        here = pl.ds(PIECES[part], PIECES[part + 1] - PIECES[part])
        return remote(
            slots.at[r, t, here],
            slots.at[r, t + 1, here],
            slot_sems.at[0, part, r, t],
            slot_sems.at[1, part, r, t + 1],
            z_ahead[r],
        )

    def trail_copy(r, t):
        return remote(
            trail_send.at[r, t],
            trail_recv.at[r, t + 1],
            trail_sems.at[0, r, t],
            trail_sems.at[1, r, t + 1],
            z_ahead[r],
        )

    every = range(len(PIECES) - 1)

    def forward(t, part):
        for r in range(2):
            slot_copy(r, t, part).start()

    loads[0].wait()
    query_flip = jnp.transpose(query_ref[...].astype(F32) * (HEAD_SIZE**-0.5))
    for r in range(2):
        slots[r, 0, 0:COLS, :] = query_flip[:, r * half : (r + 1) * half].astype(BF16)
    pl.semaphore_wait(pltpu.get_barrier_semaphore(), len(peers))
    for copy in pair_copies:
        copy.start()
    forward(0, 0)
    for load in loads[1:4]:
        load.wait()
    grad_wide = grad_ref[...].astype(F32)
    grad_flip = jnp.transpose(grad_wide)
    delta_flip = jnp.transpose(grad_wide * out_ref[...].astype(F32))
    aux_row = lax.broadcasted_iota(jnp.int32, (16, rows), 0)
    aux = jnp.zeros((16, rows), F32)
    for h in range(2):
        delta = jnp.sum(
            delta_flip[h * HEAD_SIZE : (h + 1) * HEAD_SIZE, :], axis=0, keepdims=True
        )
        for first, value in ((3 * h, stat_ref[h : h + 1, :]), (6 + 3 * h, delta)):
            rest = value
            for place in range(3):
                piece = rest.astype(BF16).astype(F32)
                aux = jnp.where(aux_row == first + place, piece, aux)
                rest = rest - piece
    for r in range(2):
        lanes = slice(r * half, (r + 1) * half)
        slots[r, 0, COLS : 2 * COLS, :] = grad_flip[:, lanes].astype(BF16)
        slots[r, 0, 2 * COLS : 2 * COLS + 16, :] = aux[:, lanes].astype(BF16)

    lane = lax.broadcasted_iota(jnp.int32, (BLOCK, COLS), 1)
    inner = lax.rem(lane, HEAD_SIZE)

    def build_keys(keys_from, values_from, base, owner):
        for b in range(blocks):
            here = slice(b * BLOCK, (b + 1) * BLOCK)
            there = slice(base + b * BLOCK, base + (b + 1) * BLOCK)
            frame = frames_ref[owner * blocks + b]
            keys = keys_from[here, :].astype(F32)
            values = values_from[here, :].astype(F32)
            for h in range(2):
                mine = (lane >= h * HEAD_SIZE) & (lane < (h + 1) * HEAD_SIZE)
                stat_at = (inner >= FRAMES + 3 * h) & (inner < FRAMES + 3 * h + 3)
                delta_at = (inner >= FRAMES + 6 + 3 * h) & (inner < FRAMES + 9 + 3 * h)
                key_more = jnp.where(inner == frame, 1.0, jnp.where(stat_at, -1.0, 0.0))
                value_more = jnp.where(delta_at, -1.0, 0.0)
                key_wide[h, there, :] = jnp.where(mine, keys, key_more).astype(BF16)
                value_wide[h, there, :] = jnp.where(mine, values, value_more).astype(BF16)
        key_flip[:, base : base + rows] = jnp.transpose(
            keys_from[...].astype(F32) * (HEAD_SIZE**-0.5)
        ).astype(BF16)

    frame_row = lax.broadcasted_iota(jnp.int32, (FRAMES, half), 0)
    frame_lane = lax.broadcasted_iota(jnp.int32, (FRAMES, half), 1)

    def prepare(t):
        for r, owner in enumerate((lax.rem(seq + 2 * (nz - t), count), lax.rem(seq + 2 * t, count))):
            first = owner * blocks + r * (blocks // 2)
            seen = jnp.full((FRAMES, half), frames_ref[first + blocks // 2 - 1], jnp.int32)
            for i in range(blocks // 2 - 2, -1, -1):
                seen = jnp.where(frame_lane < (i + 1) * BLOCK, frames_ref[first + i], seen)
            hidden = jnp.where(frame_row > seen, HIDDEN, 0.0).astype(BF16)
            extra = jnp.concatenate(
                [hidden, slots[r, t, 2 * COLS : 2 * COLS + 16, :], jnp.zeros((16, half), BF16)],
                axis=0,
            )
            zero = jnp.zeros((HEAD_SIZE, half), BF16)
            for which in range(2):
                low = slots[r, t, which * COLS : which * COLS + HEAD_SIZE, :]
                high = slots[r, t, which * COLS + HEAD_SIZE : (which + 1) * COLS, :]
                fixed[r, 2 * which, :, :] = jnp.concatenate([low, extra], axis=0)
                fixed[r, 2 * which + 1, :, :] = jnp.concatenate([extra, high], axis=0)
                paired[r, which, :, :] = jnp.concatenate(
                    [
                        jnp.concatenate([low, zero], axis=1),
                        jnp.concatenate([zero, high], axis=1),
                    ],
                    axis=0,
                )

    def tile(r, start):
        here = pl.ds(start, CHUNK)
        probs, scores = [], []
        for h in range(2):
            score = dot(key_wide[h, here, :], fixed[r, h, :, :])
            prob = jnp.exp2(score * LOG2E)
            prob_grad = dot(value_wide[h, here, :], fixed[r, 2 + h, :, :])
            score_grad = (prob * prob_grad).astype(BF16)
            score_low[r, h, here, :] = score_grad
            probs.append(prob.astype(BF16))
            scores.append(score_grad)
        value_sum[here, :] += dot_nt(jnp.concatenate(probs, axis=1), paired[r, 1, :, :])
        key_sum[here, :] += dot_nt(jnp.concatenate(scores, axis=1), paired[r, 0, :, :])

    def tiles(first):
        for c in range(rows // CHUNK):
            for r in range(2):
                tile(r, first + c * CHUNK)

    def query_part(r, first, length):
        return jnp.concatenate(
            [
                dot(
                    key_flip[h * HEAD_SIZE : (h + 1) * HEAD_SIZE, first : first + length],
                    score_low[r, h, first : first + length, :],
                )
                for h in range(2)
            ],
            axis=0,
        )

    def pass_on(t, parts, onward=None):
        for part in parts:
            for r in range(2):
                slot_copy(r, t - 1, part).wait_recv()
                if onward is None:

                    @pl.when(t < nz - 1)
                    def _(r=r, part=part):
                        slot_copy(r, t, part).start()

                elif onward:
                    slot_copy(r, t, part).start()

    def hand_on(t, totals):
        if not isinstance(t, int) or t > 1:
            for r in range(2):
                trail_copy(r, t - 1).wait_recv()

        for r in range(2):
            total = totals[r] + trail_recv[r, t, :, :].astype(F32)
            trail_send[r, t, :, :] = total.astype(BF16)
            trail_copy(r, t).start()

    early = min(2, nz - 1)
    forward(0, 1)
    for load in loads[7:]:
        load.start()
    for load in loads[4:7]:
        load.wait()
    build_keys(key_ref, value_ref, 0, seq)
    key_sum[...] = jnp.zeros_like(key_sum)
    value_sum[...] = jnp.zeros_like(value_sum)
    for r in range(2):
        trail_recv[r, 1, :, :] = jnp.zeros((COLS, half), BF16)

    def own_step(t, carry):
        @pl.when(t > 0)
        def _():
            pass_on(t, every)

        prepare(t)
        tiles(0)
        for r in range(2):
            early_query[r, t, :, :] = query_part(r, 0, rows)
        return carry

    lax.fori_loop(0, early, own_step, 0)
    for copy in pair_copies:
        copy.wait()
    build_keys(key_other, value_other, rows, partner_seq)

    def other_step(t):
        prepare(t)
        tiles(rows)
        return [early_query[r, t, :, :] + query_part(r, rows, rows) for r in range(2)]

    hand_on(1, other_step(1))
    pass_on(2, every, True)

    def step(t, carry):
        @pl.when(t > early)
        def _():
            pass_on(t, every[1:])

        prepare(t)
        tiles(0)
        tiles(rows)
        pass_on(t + 1, every[:1])
        hand_on(t, [query_part(r, 0, 2 * rows) for r in range(2)])
        return carry

    lax.fori_loop(early, early + 1, step, 0)
    for r, total in enumerate(other_step(0)):
        early_query[r, 0, :, :] = total
    lax.fori_loop(early + 1, nz - 1, step, 0)
    last = nz - 1
    for load in loads[7:]:
        load.wait()
    pass_on(last, every[1:], False)
    prepare(last)
    part_copies = []
    for c in range(rows // CHUNK):
        here = slice(c * CHUNK, (c + 1) * CHUNK)
        for r in range(2):
            tile(r, rows + c * CHUNK)
        for m, total in enumerate((key_sum, value_sum)):
            part_send[m, here, :] = total[rows + c * CHUNK : rows + (c + 1) * CHUNK, :].astype(BF16)
            copy = remote(
                part_send.at[m, pl.ds(c * CHUNK, CHUNK)],
                part_recv.at[m, pl.ds(c * CHUNK, CHUNK)],
                part_sems.at[0, m, c],
                part_sems.at[1, m, c],
                partner,
            )
            copy.start()
            part_copies.append(copy)
    tiles(0)
    hand_on(last, [query_part(r, 0, 2 * rows) for r in range(2)])
    started = list(part_copies)

    for r in range(2):
        trail_copy(r, nz - 1).wait_recv()
        lanes = slice(r * half, (r + 1) * half)
        low = (early_query[r, 0, :, :] + trail_recv[r, nz, :, :].astype(F32)).astype(BF16)
        flipped_ref[0:COLS, lanes] = low
        grads_ref[lanes, 0:COLS] = jnp.transpose(low.astype(F32)).astype(BF16)

    def launch(copy):
        copy.start()
        started.append(copy)
        return copy

    def at(r, distance):
        return lax.rem(z + distance if r == 0 else z + nz - distance, nz)

    def half_of(r, i):
        return (i + r) % 2

    kinds = (
        (slice(0, COLS), zq_term, zq_send, zq_recv, zq_last),
        (slice(COLS, 3 * COLS), zk_term, zk_send, zk_recv, zk_last),
    )
    z_copies = {}

    def weight_term(kind, z_at, side_at):
        first = pl.multiple_of((z_at * 2 + side_at) * COLS, COLS)
        return dot(flipped_ref[kinds[kind][0], :], input_ref[:, pl.ds(first, COLS)])

    def z_term(kind, i):
        for r in range(2):
            kinds[kind][1][r, i, :, :] = weight_term(kind, at(r, (nz - i) // 2), half_of(r, i))

    def z_message(kind, i, ready=False):
        _, term, send, recv, final = kinds[kind]
        if not ready:
            z_term(kind, i)
        for r in range(2):
            total = term[r, i, :, :]
            if i >= 2:
                z_copies[kind, r, i - 2].wait_recv()
                total = total + recv[r, i - 2, :, :].astype(F32)
            send[r, i, :, :] = total.astype(BF16)
            if i < nz - 3:
                copy = remote(
                    send.at[r, i],
                    recv.at[r, i],
                    z_sems.at[kind, 0, r, i],
                    z_sems.at[kind, 1, r, i],
                    z_ahead[r],
                )
            else:
                copy = remote(
                    send.at[r, i],
                    final.at[r, side],
                    z_sems.at[kind, 0, r, i],
                    last_sems.at[kind, r, side],
                    {"seq": 2 * at(r, 1) + half_of(r, i)},
                )
            z_copies[kind, r, i] = launch(copy)

    near_copies = {}

    def z_near(kind):
        rows_of = kinds[kind][0]
        near_send[rows_of, :] = weight_term(kind, z, 1 - side).astype(BF16)
        near_copies[kind] = launch(
            remote(
                near_send.at[rows_of],
                near_recv.at[rows_of],
                near_sems.at[0, kind],
                near_sems.at[1, kind],
                partner,
            )
        )
        near_term[rows_of, :] = weight_term(kind, z, side)

    def z_final(kind):
        rows_of, _, send, _, final = kinds[kind]
        near_copies[kind].wait_recv()
        total = near_term[rows_of, :] + near_recv[rows_of, :].astype(F32)
        for r in range(2):
            for source in range(2):
                remote(
                    send.at[r, 0],
                    final.at[r, source],
                    z_sems.at[kind, 0, r, 0],
                    last_sems.at[kind, r, source],
                    partner,
                ).wait_recv()
                total = total + final[r, source, :, :].astype(F32)
        for place in range(total.shape[0] // COLS):
            m = rows_of.start // COLS + place
            weight_out[m, :, :] = jnp.transpose(total[place * COLS : (place + 1) * COLS, :])

    def input_term(dx, core_at):
        weights = []
        for y_at in range(2):
            first = pl.multiple_of(((y_at * nx + lax.rem(x + dx, nx)) * 2 + core_at) * COLS, COLS)
            weights.append(
                jnp.concatenate([weight_ref[m, pl.ds(first, COLS), :] for m in range(3)], axis=1)
            )
        return dot_nt(grads_ref[...], jnp.concatenate(weights, axis=0))

    core_copies = {}

    def core_message(dx):
        core_send[dx, :, :] = input_term(dx, 1 - core).astype(BF16)
        core_copies[dx] = launch(
            remote(
                core_send.at[dx],
                core_recv.at[dx],
                core_sems.at[0, dx],
                core_sems.at[1, dx],
                twin,
            )
        )

    x_copies = {}
    fourth = half // 2

    def x_message(kind, r, i):
        send, recv, sems = ((xa_send, xa_recv, xa_sems), (xb_send, xb_recv, xb_sems))[kind]
        x_copies[kind, r, i] = launch(
            remote(send.at[r, i], recv.at[r, i], sems.at[0, r, i], sems.at[1, r, i], x_ahead[r])
        )

    y_copies = {}

    def x_pair(dx):
        total = input_term(dx, core)
        core_copies[dx].wait_recv()
        total = total + core_recv[dx, :, :].astype(F32)
        sides = [total[:, y_at * COLS : (y_at + 1) * COLS] for y_at in range(2)]
        for r in range(2):
            if dx == 2:
                xa_send[r, 0, :, :] = sides[r][:half, :].astype(BF16)
                x_message(0, r, 0)
            elif dx == (1, nx - 1)[r]:
                xa_send[r, 1, :, :] = sides[1 - r][:half, :].astype(BF16)
                x_message(0, r, 1)
                xa_term[r, :, :] = sides[r][:half, :]
            elif dx == 0:
                xa_own[r, :, :] = sides[r][:half, :]
        low, high = sides[0][half:, :], sides[1][half:, :]
        yb_send[dx, :, :] = jnp.where(low_side == 0, high, low).astype(BF16)
        yb_term[dx, :, :] = jnp.where(low_side == 0, low, high)
        y_copies[dx] = launch(
            remote(
                yb_send.at[dx], yb_recv.at[dx], y_sems.at[0, dx], y_sems.at[1, dx], neighbour
            )
        )

    def xa_third(r):
        x_copies[0, r, 0].wait_recv()
        xa_send[r, 2, :, :] = (xa_term[r, :, :] + xa_recv[r, 0, :, :].astype(F32)).astype(BF16)
        x_message(0, r, 2)

    def xb_block(dx):
        y_copies[dx].wait_recv()
        yb_term[dx, :, :] += yb_recv[dx, :, :].astype(F32)

    def xb_part(dx, part):
        return yb_term[dx, part * fourth : (part + 1) * fourth, :]

    def xb_first():
        xb_block(2)
        for r in range(2):
            xb_send[r, 0, :, :] = xb_part(2, r).astype(BF16)
            x_message(1, r, 0)

    def xb_second(r):
        dx = (1, nx - 1)[r]
        xb_block(dx)
        xb_send[r, 1, :, :] = xb_part(dx, 1 - r).astype(BF16)
        x_message(1, r, 1)

    def xb_third(r):
        x_copies[1, r, 0].wait_recv()
        total = xb_part((1, nx - 1)[r], r) + xb_recv[r, 0, :, :].astype(F32)
        xb_send[r, 2, :, :] = total.astype(BF16)
        x_message(1, r, 2)

    def xb_final():
        for part in range(2):
            total = xb_part(0, part)
            for r in range(2):
                i = 2 if r == part else 1
                x_copies[1, r, i].wait_recv()
                total = total + xb_recv[r, i, :, :].astype(F32)
            input_out[half + part * fourth : half + (part + 1) * fourth, :] = total.astype(BF16)

    def xa_final():
        totals = []
        for y_at in range(2):
            total = xa_own[y_at, :, :]
            for r in range(2):
                i = 2 if r == y_at else 1
                x_copies[0, r, i].wait_recv()
                total = total + xa_recv[r, i, :, :].astype(F32)
            totals.append(total)
        ya_send[...] = jnp.where(low_side == 0, totals[1], totals[0]).astype(BF16)
        xa_own[0, :, :] = jnp.where(low_side == 0, totals[0], totals[1])
        return launch(
            remote(ya_send, ya_recv, y_sems.at[0, nx], y_sems.at[1, nx], neighbour)
        )

    def drain(t, carry):
        for r in range(2):
            for part in every:
                slot_copy(r, t, part).wait_send()
            trail_copy(r, t + 1).wait_send()
        return carry

    z_message(0, 0)
    z_message(0, 1)
    for c in range(rows // CHUNK):
        here = slice(c * CHUNK, (c + 1) * CHUNK)
        for m, total in ((1, key_sum), (2, value_sum)):
            part_copies[2 * c + m - 1].wait_recv()
            low = (total[here, :] + part_recv[m - 1, here, :].astype(F32)).astype(BF16)
            grads_ref[here, m * COLS : (m + 1) * COLS] = low
            flipped_ref[m * COLS : (m + 1) * COLS, here] = jnp.transpose(
                low.astype(F32)
            ).astype(BF16)
    core_message(2)
    core_message(3)
    z_message(1, 0)
    core_message(1)
    z_message(1, 1)
    x_pair(2)
    core_message(0)
    z_term(1, 2)
    z_message(0, 2)
    x_pair(3)
    z_near(1)
    z_near(0)
    z_message(1, 2, True)
    x_pair(1)
    z_term(1, 4)
    z_message(0, 3)
    z_term(1, 6)
    z_term(1, 3)
    xa_third(0)
    xa_third(1)
    z_term(1, 5)
    xb_first()
    z_message(1, 3, True)
    xb_second(1)
    x_pair(0)
    z_message(0, 4)
    z_message(0, 5)
    z_message(1, 4, True)
    y_copy = xa_final()
    xb_second(0)
    z_message(1, 5, True)
    z_message(0, 6)
    xb_block(0)
    xb_third(0)
    xb_third(1)
    z_message(1, 6, True)
    y_copy.wait_recv()
    input_out[0:half, :] = (xa_own[0, :, :] + ya_recv[...].astype(F32)).astype(BF16)
    z_final(0)
    xb_final()
    z_final(1)
    lax.fori_loop(0, nz - 1, drain, 0)
    for copy in started:
        copy.wait_send()


def local(
    nz,
    nx,
    layer_input,
    qkv_weight,
    queries,
    key_states,
    value_states,
    attn_out,
    grad_out,
    log_sum_exp,
    frames,
):
    rows = queries.shape[0]
    half = rows // 2
    wide = 3 * COLS
    vmem = pl.BlockSpec(memory_space=pltpu.VMEM)
    anywhere = pl.BlockSpec(memory_space=pltpu.HBM)
    dma = pltpu.SemaphoreType.DMA
    stat = log_sum_exp.T

    def low(*shape):
        return pltpu.VMEM(shape, BF16)

    def full(*shape):
        return pltpu.VMEM(shape, F32)

    return pl.pallas_call(
        functools.partial(backward_kernel, nz, nx),
        out_shape=(
            pltpu.VMEM((rows, COLS), BF16),
            pltpu.VMEM((3, COLS, COLS), F32),
        ),
        in_specs=[anywhere] * 9,
        out_specs=(vmem, vmem),
        scratch_shapes=[
            pltpu.SMEM(frames.shape, jnp.int32),
            full(*stat.shape),
            low(rows, COLS),
            low(rows, COLS),
            low(rows, COLS),
            low(rows, COLS),
            low(rows, COLS),
            low(*layer_input.shape),
            low(*qkv_weight.shape),
            low(rows, COLS),
            low(rows, COLS),
            low(2, nz, 2 * COLS + 16, half),
            low(2, nz, COLS, half),
            low(2, nz + 1, COLS, half),
            low(2, 2 * rows, COLS),
            low(2, 2 * rows, COLS),
            low(COLS, 2 * rows),
            low(2, 4, COLS, half),
            low(2, 2, COLS, 2 * half),
            low(2, 2, 2 * rows, half),
            full(2 * rows, COLS),
            full(2 * rows, COLS),
            full(2, 2, COLS, half),
            low(2, rows, COLS),
            low(2, rows, COLS),
            low(rows, wide),
            low(wide, rows),
            low(nx, rows, 2 * COLS),
            low(nx, rows, 2 * COLS),
            low(2, 3, half, COLS),
            low(2, 3, half, COLS),
            full(2, half, COLS),
            full(2, half, COLS),
            low(2, 3, half // 2, COLS),
            low(2, 3, half // 2, COLS),
            low(nx, half, COLS),
            low(nx, half, COLS),
            full(nx, half, COLS),
            low(half, COLS),
            low(half, COLS),
            full(2, nz - 1, COLS, COLS),
            low(2, nz - 1, COLS, COLS),
            low(2, nz - 3, COLS, COLS),
            low(2, 2, COLS, COLS),
            full(2, nz - 1, 2 * COLS, COLS),
            low(2, nz - 1, 2 * COLS, COLS),
            low(2, nz - 3, 2 * COLS, COLS),
            low(2, 2, 2 * COLS, COLS),
            full(wide, COLS),
            low(wide, COLS),
            low(wide, COLS),
            dma((9,)),
            dma((2, len(PIECES) - 1, 2, nz)),
            dma((2, 2, nz + 1)),
            dma((2, 2)),
            dma((2, 2, rows // CHUNK)),
            dma((2, nx)),
            dma((2, 2, 3)),
            dma((2, 2, 3)),
            dma((2, nx + 1)),
            dma((2, 2, 2, nz - 1)),
            dma((2, 2, 2)),
            dma((2, 2)),
        ],
        compiler_params=pltpu.CompilerParams(
            collective_id=0, has_side_effects=True, vmem_limit_bytes=48 * 2**20
        ),
        name="attention_backward",
    )(
        *(
            pltpu.with_memory_space_constraint(array, pltpu.HBM)
            for array in (
                frames,
                stat,
                queries,
                key_states,
                value_states,
                attn_out,
                grad_out,
                layer_input,
                qkv_weight,
            )
        )
    )


def solution(mesh):
    nz = mesh.shape["seq"] // 2
    nx = mesh.shape["head"] // 4
    placed = (
        P("seq", None),
        P(None, None, "head"),
        P("seq", "head"),
        P("seq", "head"),
        P("seq", "head"),
        P("seq", "head"),
        P("seq", "head"),
        P("seq", "head"),
        P(),
    )
    return jax.shard_map(
        functools.partial(local, nz, nx),
        mesh=mesh,
        in_specs=placed,
        out_specs=(P("seq", "head"), P(None, "seq", "head")),
        check_vma=False,
    )
```
